32 devices in a mesh: rows: 4 (over z), centers: 8 (over y, x, core).
Axes of the slice: x: 2, y: 2, z: 4, core: 2. Of those that a mesh axis runs over, the one named last changes fastest.
Arguments:
- features: float32 [4096, 128], P('rows'), may hold values from -6 to 6
- centers: float32 [16384, 128], P('centers'), may hold values from -6 to 6
- labels: int32 [4096, 64], P('rows'), may hold values 0 or 1
- coeffs: float32 [16384, 64], P('centers'), may hold values from -3 to 3
- precond: float32 [16384, 16384], P('rows', 'centers'), may hold values from -2 to 2, as said below
Outputs:
- coeffs_out: float32 [16384, 64], P('centers')
The draws below stay inside these ranges and needn't reach their ends.
Inputs may be any that keep to these rules, and one draw needn't show every extreme that they name: precond is lower triangular: every entry above the diagonal is zero, and its diagonal is positive.
All inputs are finite; a program needn't handle non-finite values. No bound on the sum of `labels` on one device may be relied on, other than what follows from the above.
Results may differ from the reference program's by a relative error of at most 0.0003.
Values sent between devices are 32-bit elements; how exact they have to be, the bound alone decides.
No kernel may reach another device: no remote copies, remote signals or barrier semaphores. Data moves between devices by JAX's collectives and lax.ppermute only.
A program may use at most 128 MiB of HBM per device.

```python
import jax
import jax.numpy as jnp
from jax import lax

D = 128
M = 16384
OUT = 64
STEPS = 2
ROWS_ALL = 4096


def draw_precond(key, part):
    first = jax.random.fold_in(key, 11)
    second = jax.random.fold_in(key, 23)
    lower = jnp.clip(jax.random.normal(first, (M, M), jnp.float32), -6.0, 6.0) * (1.5 / jnp.sqrt(jnp.float32(M)))
    diag_vals = jnp.exp(jax.random.uniform(second, (M,), jnp.float32, jnp.log(0.5), jnp.log(2.0)))
    return jnp.tril(lower, -1) + jnp.diag(diag_vals)


def place_ends(drawn, key, least, top_value):
    shape = drawn.shape
    place = [jax.random.randint(jax.random.fold_in(key, axis), (), 0, shape[axis]) for axis in range(len(shape))]
    drawn = drawn.at[tuple(place)].set(least)
    longest = shape.index(max(shape))
    place[longest] = (place[longest] + 1) % shape[longest]
    return drawn.at[tuple(place)].set(top_value)


def levels(key, shape, shards, least, top_value):
    def one(position, blocks):
        heights = jax.random.uniform(jax.random.fold_in(jax.random.fold_in(key, 6), position), (blocks,), jnp.float32, least / len(shards), top_value / len(shards))
        return jnp.repeat(jnp.exp(heights), shape[position] // blocks).reshape((-1,) + (1,) * (len(shape) - position - 1))

    gain = one(*shards[0])
    for cut in shards[1:]:
        gain = gain * one(*cut)
    return gain


def scatter_about(key, shape, spread, limit, shards=(), kind=jnp.bfloat16):
    factor_of = levels(key, shape, shards, -0.22, 0.18) if shards else 1.0
    result = jax.random.normal(key, shape, jnp.float32) * spread * factor_of
    return jnp.minimum(jnp.maximum(result, -limit), limit).astype(kind)


def setup_inputs(seed: int = 0) -> dict:
    seeds = jax.random.split(jax.random.key(seed), 6)
    return {
        "features": scatter_about(seeds[0], (ROWS_ALL, D), 1.0, 6.0, ((0, 4),), jnp.float32),
        "centers": scatter_about(seeds[1], (M, D), 1.0, 6.0, ((0, 8),), jnp.float32),
        "labels": place_ends((jax.random.randint(seeds[2], (ROWS_ALL, OUT), 0, 2) < 1).astype(jnp.int32), jax.random.fold_in(seeds[2], 1), 0, 1),
        "coeffs": scatter_about(seeds[3], (M, OUT), 0.5, 3.0, ((0, 8),), jnp.float32),
        "precond": draw_precond(jax.random.fold_in(seeds[5], 71), 0),
    }


def kernel_tile(rows_x, centers_x):
    width = rows_x.shape[1]
    left = lax.optimization_barrier(jnp.sum(rows_x * rows_x, axis=1))
    right = lax.optimization_barrier(jnp.sum(centers_x * centers_x, axis=1))
    cross = jnp.dot(rows_x, centers_x.T, precision=lax.Precision.HIGHEST)
    return jnp.exp(-2.0 * (left[:, None] + right[None, :] - 2.0 * cross) / width)

def reference(features, centers, labels, coeffs, precond):
    rows_total = features.shape[0]
    block = min(1024, rows_total)
    blocks = rows_total // block
    targets = labels.astype(jnp.float32)
    for step in range(STEPS):

        def accumulate(total, index):
            start = (index * block).astype(jnp.int32)
            rows_x = lax.dynamic_slice_in_dim(features, start, block, 0)
            rows_y = lax.dynamic_slice_in_dim(targets, start, block, 0)
            tile = kernel_tile(rows_x, centers)
            logits = jnp.dot(tile, coeffs, precision=lax.Precision.HIGHEST)
            resid = (jax.nn.sigmoid(logits) - rows_y) / rows_total
            return (total + jnp.dot(tile.T, resid, precision=lax.Precision.HIGHEST), None)
        grad, unused = lax.scan(accumulate, jnp.zeros(coeffs.shape, jnp.float32), jnp.arange(blocks, dtype=jnp.int32))
        fwd = jnp.dot(precond, grad, precision=lax.Precision.HIGHEST)
        back = jnp.dot(precond.T, fwd, precision=lax.Precision.HIGHEST)
        total = jnp.sum(fwd * fwd)
        scale = 0.5 / jnp.sqrt(total / (fwd.shape[0] * fwd.shape[1]) + 1e-06)
        coeffs = coeffs - scale * back
    return coeffs
```

```python
import functools

import jax
import jax.numpy as jnp
from jax import lax
from jax.experimental import pallas as pl
from jax.experimental.pallas import tpu as pltpu
from jax.sharding import PartitionSpec as P

STEPS = 2
step_size = 0.5
epsilon = 1e-06

f32 = jnp.float32
bf16 = jnp.bfloat16
LOG2E = 1.4426950408889634
NN = (((1,), (0,)), ((), ()))
NT = (((1,), (1,)), ((), ()))
WHOLE = pl.BlockSpec(memory_space=pltpu.VMEM)
VMEM_LIMIT = 30 << 20
SLOTS = 6


def dot(a, b, dims):
    return lax.dot_general(a, b, dims, preferred_element_type=f32)


def split(x):
    high = x.astype(bf16)
    return high, (x - high.astype(f32)).astype(bf16)


def split3(x):
    high = x.astype(bf16)
    rest = x - high.astype(f32)
    mid = rest.astype(bf16)
    return high, mid, (rest - mid.astype(f32)).astype(bf16)


def core_of():
    return lax.rem(lax.axis_index("centers"), 2)


def chip_of():
    return lax.div(lax.axis_index("centers"), 2)


def rows_at(start, count):
    return pl.ds(pl.multiple_of(start, count), count)


def stage(x_ref, pieces, places, full, parts):
    for piece, (start, lanes) in zip(pieces, places()):
        full[rows_at(start, piece.shape[0]), lanes] = piece[...]
    high, low = split(full[...])
    out = full.shape[0]
    parts[0:out] = high
    parts[out : 2 * out] = low


def stream(count, copy, use):
    slots = min(SLOTS, count)
    for i in range(slots):
        copy(i, i).start()

    def one(i, carry):
        slot = lax.rem(i, slots)
        copy(i, slot).wait()
        use(i, slot)

        @pl.when(i + slots < count)
        def _():
            copy(i + slots, slot).start()

        return carry

    lax.fori_loop(0, count, one, 0)


def block_of(total, most):
    size = min(total, most)
    while total % size:
        size //= 2
    return size


def down(weights, pieces, places, out, chunks, chunk_at, first, count, squares, name):
    depth = weights.shape[0]
    size = block_of(depth, 512)
    n_pieces = len(pieces)
    share = out // chunks
    extra = 128 if squares else 0

    def kernel(*refs):
        piece_refs = refs[:n_pieces]
        w_ref = refs[n_pieces]
        outs = refs[n_pieces + 1 : n_pieces + 1 + chunks]
        full, parts, total, held, sems = refs[n_pieces + 1 + chunks :]

        def copy(i, slot):
            return pltpu.make_async_copy(
                w_ref.at[pl.ds(i * size, size), pl.ds(first, count)], held.at[slot], sems.at[slot]
            )

        def use(i, slot):
            x = parts[:, pl.ds(pl.multiple_of(i * size, size), size)]
            high, low = split(held[slot])
            both = dot(x, high, NN)
            total[...] += both[:out] + both[out:] + dot(x[:out], low, NN)

        total[...] = jnp.zeros_like(total)
        stage(None, piece_refs, places, full, parts)
        stream(depth // size, copy, use)
        for k in range(chunks):
            outs[k][:, 0:count] = total[rows_at(chunk_at(k) * share, share), :]
        if squares:
            sum_sq = jnp.sum(full[...] * full[...])
            for k in range(chunks):
                outs[k][:, count : count + extra] = jnp.full((share, extra), sum_sq, f32)

    slots = min(SLOTS, depth // size)
    return pl.pallas_call(
        kernel,
        in_specs=[WHOLE] * n_pieces + [pl.BlockSpec(memory_space=pl.ANY)],
        out_specs=[WHOLE] * chunks,
        out_shape=[jax.ShapeDtypeStruct((share, count + extra), f32)] * chunks,
        scratch_shapes=[
            pltpu.VMEM((out, depth), f32),
            pltpu.VMEM((2 * out, depth), bf16),
            pltpu.VMEM((out, count), f32),
            pltpu.VMEM((slots, size, count), f32),
            pltpu.SemaphoreType.DMA((slots,)),
        ],
        compiler_params=pltpu.CompilerParams(vmem_limit_bytes=VMEM_LIMIT),
        cost_estimate=pl.CostEstimate(
            flops=6 * out * depth * count, bytes_accessed=4 * depth * count, transcendentals=0
        ),
        name=name,
    )(*pieces, weights)


def across(weights, pieces, places, out, first, count, name):
    width = weights.shape[1]
    size = block_of(count, 512)
    n_pieces = len(pieces)
    half = out // 2

    def kernel(*refs):
        piece_refs = refs[:n_pieces]
        w_ref, theirs, mine, full, parts, total, held, sems = refs[n_pieces:]

        def copy(i, slot):
            return pltpu.make_async_copy(w_ref.at[pl.ds(first + i * size, size)], held.at[slot], sems.at[slot])

        def use(i, slot):
            high, low = split(held[slot])
            both = dot(parts[...], high, NT)
            at = pl.ds(pl.multiple_of(i * size, size), size)
            total[:, at] = both[:out] + both[out:] + dot(parts[0:out], low, NT)

        stage(None, piece_refs, places, full, parts)
        stream(count // size, copy, use)
        core = core_of()
        theirs[...] = total[rows_at((1 - core) * half, half), :]
        mine[...] = total[rows_at(core * half, half), :]

    slots = min(SLOTS, count // size)
    return pl.pallas_call(
        kernel,
        in_specs=[WHOLE] * n_pieces + [pl.BlockSpec(memory_space=pl.ANY)],
        out_specs=[WHOLE] * 2,
        out_shape=[jax.ShapeDtypeStruct((half, count), f32)] * 2,
        scratch_shapes=[
            pltpu.VMEM((out, width), f32),
            pltpu.VMEM((2 * out, width), bf16),
            pltpu.VMEM((out, count), f32),
            pltpu.VMEM((slots, size, width), f32),
            pltpu.SemaphoreType.DMA((slots,)),
        ],
        compiler_params=pltpu.CompilerParams(vmem_limit_bytes=VMEM_LIMIT),
        cost_estimate=pl.CostEstimate(
            flops=6 * out * width * count, bytes_accessed=4 * width * count, transcendentals=0
        ),
        name=name,
    )(*pieces, weights)


def tile_and_logits(features, centers, coeffs):
    rows, width = features.shape
    count = centers.shape[0]
    out = coeffs.shape[0]
    half = out // 2
    size = block_of(rows, 512)
    gain = 2.0 * LOG2E / width

    def kernel(x_ref, c_ref, a_ref, tile_ref, theirs, mine, wide, norms, parts, total):
        @pl.when(pl.program_id(0) == 0)
        def _():
            c = c_ref[...]
            high, mid, low = split3(c * (2.0 * gain))
            wide[...] = jnp.concatenate([high, high, mid, mid, low, high], axis=1)
            norms[...] = lax.dot_general(
                jnp.full((8, width), gain, f32),
                c * c,
                NT,
                precision=lax.Precision.HIGHEST,
                preferred_element_type=f32,
            )
            high, low = split(a_ref[...])
            parts[0:out] = high
            parts[out : 2 * out] = low

        x = x_ref[...]
        high, mid, low = split3(x)
        cross = dot(jnp.concatenate([high, mid, high, mid, high, low], axis=1), wide[...], NT)
        norm = jnp.sum(x * x, axis=1, keepdims=True) * gain
        tile = jnp.exp2((cross - norm) - norms[0:1, :])
        tile_ref[...] = tile
        high, low = split(tile)
        both = dot(parts[...], high, NT)
        total[...] = both[:out] + both[out:] + dot(parts[0:out], low, NT)
        core = core_of()
        theirs[...] = total[rows_at((1 - core) * half, half), :]
        mine[...] = total[rows_at(core * half, half), :]

    return pl.pallas_call(
        kernel,
        grid=(rows // size,),
        in_specs=[
            pl.BlockSpec((size, width), lambda i: (i, 0)),
            pl.BlockSpec((count, width), lambda i: (0, 0)),
            pl.BlockSpec((out, count), lambda i: (0, 0)),
        ],
        out_specs=[
            pl.BlockSpec((size, count), lambda i: (i, 0)),
            pl.BlockSpec((half, size), lambda i: (0, i)),
            pl.BlockSpec((half, size), lambda i: (0, i)),
        ],
        out_shape=[
            jax.ShapeDtypeStruct((rows, count), f32),
            jax.ShapeDtypeStruct((half, rows), f32),
            jax.ShapeDtypeStruct((half, rows), f32),
        ],
        scratch_shapes=[
            pltpu.VMEM((count, 6 * width), bf16),
            pltpu.VMEM((8, count), f32),
            pltpu.VMEM((2 * out, count), bf16),
            pltpu.VMEM((out, size), f32),
        ],
        compiler_params=pltpu.CompilerParams(vmem_limit_bytes=VMEM_LIMIT),
        cost_estimate=pl.CostEstimate(
            flops=12 * rows * width * count, bytes_accessed=4 * rows * count, transcendentals=rows * count
        ),
        name="tile_and_logits",
    )(features, centers, coeffs)


def add_and_cut(first, second, chips, name):
    half, count = first.shape
    share = half // chips

    def kernel(a_ref, b_ref, *outs):
        chip = chip_of()
        for k in range(chips):
            at = rows_at((chip ^ k) * share, share)
            outs[k][...] = a_ref[at, :] + b_ref[at, :]

    return pl.pallas_call(
        kernel,
        in_specs=[WHOLE] * 2,
        out_specs=[WHOLE] * chips,
        out_shape=[jax.ShapeDtypeStruct((share, count), f32)] * chips,
        name=name,
    )(first, second)


def assemble(pieces, places, shape, name):
    n_pieces = len(pieces)

    def kernel(*refs):
        for piece, (start, lanes) in zip(refs[:n_pieces], places()):
            refs[n_pieces][rows_at(start, piece.shape[0]), lanes] = piece[...]

    return pl.pallas_call(
        kernel,
        in_specs=[WHOLE] * n_pieces,
        out_specs=WHOLE,
        out_shape=jax.ShapeDtypeStruct(shape, f32),
        name=name,
    )(*pieces)


def swap(x, axis, mask):
    size = lax.axis_size(axis)
    return lax.ppermute(x, axis, [(i, i ^ mask) for i in range(size)])


def body(features, centers, labels, coeffs, precond):
    depth_ranks = lax.axis_size("rows")
    chips = lax.axis_size("centers") // 2
    rows_total = features.shape[0] * depth_ranks
    count, out = coeffs.shape
    center_total = count * lax.axis_size("centers")
    p_rows = precond.shape[0]
    half = out // 2
    share = out // depth_ranks
    part = half // chips
    cols = count // 2
    row_half = p_rows // 2

    rank = lax.axis_index("rows")
    core = core_of()
    targets = lax.dynamic_slice_in_dim(labels.T, core * half, half, 0).astype(f32)
    a = coeffs.T
    a_share = lax.dynamic_slice_in_dim(a, rank * share, share, 0)

    def rank_of(k):
        return lax.axis_index("rows") ^ k

    def core_places():
        me = core_of()
        return [(me * half, slice(None)), ((1 - me) * half, slice(None))]

    def rank_places():
        return [(rank_of(k) * share, slice(None)) for k in range(depth_ranks)]

    def rank_places_cols():
        return [
            (rank_of(k) * share, slice(h * cols, (h + 1) * cols)) for h in range(2) for k in range(depth_ranks)
        ]

    def fwd_places():
        me, chip = core_of(), chip_of()
        return [
            (who * half + (chip ^ k) * part, slice(h * row_half, (h + 1) * row_half))
            for h in range(2)
            for who in (me, 1 - me)
            for k in range(chips)
        ]

    a_pieces = None
    for step in range(STEPS):
        if step == 0:
            tile, theirs, mine = tile_and_logits(features, centers, a)
        else:
            theirs, mine = across(tile, a_pieces, rank_places_cols, out, 0, tile.shape[0], "logits")
        logits = mine + swap(theirs, "centers", 1)
        full = logits
        for k in range(1, chips):
            full = full + swap(logits, "centers", 2 * k)
        resid = (jax.nn.sigmoid(full) - targets) / rows_total
        cuts = down(
            tile, [resid, swap(resid, "centers", 1)], core_places, out, depth_ranks, rank_of, 0, count, False, "grad"
        )
        grad = cuts[0]
        for k in range(1, depth_ranks):
            grad = grad + swap(cuts[k], "rows", k)
        grads = [grad] + [swap(grad, "rows", k) for k in range(1, depth_ranks)]
        fwd = []
        for h in range(2):
            theirs, mine = across(precond, grads, rank_places, out, h * row_half, row_half, f"fwd{'ab'[h]}")
            cuts = add_and_cut(mine, swap(theirs, "centers", 1), chips, f"cut{'ab'[h]}")
            total = cuts[0]
            for k in range(1, chips):
                total = total + swap(cuts[k], "centers", 2 * k)
            own = [total] + [swap(total, "centers", 2 * k) for k in range(1, chips)]
            other = swap(jnp.concatenate(own, axis=0), "centers", 1)
            fwd += own + [other[k * part : (k + 1) * part] for k in range(chips)]
        scale = None
        updated = []
        for h in range(2):
            cuts = down(
                precond, fwd, fwd_places, out, depth_ranks, rank_of, h * cols, cols, h == 0, f"back{'ab'[h]}"
            )
            back = cuts[0]
            for k in range(1, depth_ranks):
                back = back + swap(cuts[k], "rows", k)
            if h == 0:
                scale = step_size / jnp.sqrt(back[0, cols] / (center_total * out) + epsilon)
                back = back[:, :cols]
            updated.append(a_share[:, h * cols : (h + 1) * cols] - scale * back)
        a_pieces = [u if k == 0 else swap(u, "rows", k) for u in updated for k in range(depth_ranks)]
        a_share = jnp.concatenate(updated, axis=1)
    return assemble(a_pieces, rank_places_cols, (out, count), "result").T


def plain_tile(rows_x, centers_x):
    width = rows_x.shape[1]
    left = jnp.sum(rows_x * rows_x, axis=1)
    right = jnp.sum(centers_x * centers_x, axis=1)
    cross = jnp.dot(rows_x, centers_x.T, precision=lax.Precision.HIGHEST)
    return jnp.exp(-2.0 * (left[:, None] + right[None, :] - 2.0 * cross) / width)


def plain_body(features, centers, labels, coeffs, precond):
    rows_total = features.shape[0] * lax.axis_size("rows")
    center_total = coeffs.shape[0] * lax.axis_size("centers")
    targets = labels.astype(f32)
    share_rows = features.shape[0] // lax.axis_size("centers")
    highest = lax.Precision.HIGHEST
    tile = plain_tile(features, centers)
    for step in range(STEPS):
        part = jnp.dot(tile, coeffs, precision=highest)
        share = lax.psum_scatter(part, "centers", scatter_dimension=0, tiled=True)
        offset = lax.axis_index("centers") * share_rows
        share_y = lax.dynamic_slice_in_dim(targets, offset, share_rows, 0)
        share_resid = (jax.nn.sigmoid(share) - share_y) / rows_total
        resid = lax.all_gather(share_resid, "centers", axis=0, tiled=True)
        grad = lax.psum(lax.dot_general(tile, resid, (((0,), (0,)), ((), ())), precision=highest), "rows")
        fwd = lax.psum(jnp.dot(precond, grad, precision=highest), "centers")
        back = lax.psum(lax.dot_general(precond, fwd, (((0,), (0,)), ((), ())), precision=highest), "rows")
        total = lax.psum(jnp.sum(fwd * fwd), "rows")
        scale = step_size / jnp.sqrt(total / (center_total * fwd.shape[1]) + epsilon)
        coeffs = coeffs - scale * back
    return coeffs


def fits(ranks, cols, features, coeffs, precond):
    if cols % 2 or ranks & (ranks - 1) or cols & (cols - 1):
        return False
    out = coeffs.shape[1]
    lanes = (features.shape[0] // ranks, coeffs.shape[0] // cols // 2, precond.shape[0] // ranks // 2)
    return out % (8 * ranks) == 0 and out % (8 * cols) == 0 and all(n % 128 == 0 for n in lanes)


def solution(mesh):
    in_specs = (
        P("rows", None),
        P("centers", None),
        P("rows", None),
        P("centers", None),
        P("rows", "centers"),
    )
    out_specs = P("centers", None)

    def program(features, centers, labels, coeffs, precond):
        fit = fits(mesh.shape["rows"], mesh.shape["centers"], features, coeffs, precond)
        one = jax.shard_map(
            body if fit else plain_body, mesh=mesh, in_specs=in_specs, out_specs=out_specs, check_vma=False
        )
        return one(features, centers, labels, coeffs, precond)

    return program
```

```python
import functools

import jax
import jax.numpy as jnp
from jax import lax
from jax.experimental import pallas as pl
from jax.experimental.pallas import tpu as pltpu
from jax.sharding import PartitionSpec as P

STEPS = 2
step_size = 0.5
epsilon = 1e-06

f32 = jnp.float32
bf16 = jnp.bfloat16
LOG2E = 1.4426950408889634
NN = (((1,), (0,)), ((), ()))
NT = (((1,), (1,)), ((), ()))
WHOLE = pl.BlockSpec(memory_space=pltpu.VMEM)
FAR = pl.BlockSpec(memory_space=pltpu.HBM)
VMEM_LIMIT = 26 << 20
TILE_LIMIT = 62 << 20
NEAR_LIMIT = 26 << 20
SMALL_LIMIT = 8 << 20
IN_FLIGHT = 12 << 20


def dot(a, b, dims):
    return lax.dot_general(a, b, dims, preferred_element_type=f32)


def split(x):
    high = x.astype(bf16)
    return high, (x - high.astype(f32)).astype(bf16)


def split3(x):
    high = x.astype(bf16)
    rest = x - high.astype(f32)
    mid = rest.astype(bf16)
    return high, mid, (rest - mid.astype(f32)).astype(bf16)


def core_of():
    return lax.rem(lax.axis_index("centers"), 2)


def chip_of():
    return lax.div(lax.axis_index("centers"), 2)


def rows_at(start, count):
    return pl.ds(pl.multiple_of(start, count), count)


def stage(pieces, places, full, parts):
    for piece, (start, lanes) in zip(pieces, places()):
        full[rows_at(start, piece.shape[0]), lanes] = piece[...]
    high, low = split(full[...])
    out = full.shape[0]
    parts[0:out] = high
    parts[out : 2 * out] = low


def block_of(total, most):
    size = min(total, most)
    while total % size:
        size //= 2
    return size


def offset(first, size):
    return first if isinstance(first, int) else pl.multiple_of(first(), size)


def stream(w_ref, held, sems, first, count, size, lanes, use):
    blocks = count // size
    start = offset(first, size)

    def at(i):
        return pl.ds(pl.multiple_of(i * size, size), size)

    def rows(i):
        return pl.ds(pl.multiple_of(start + i * size, size), size)

    def copy(i, slot):
        return pltpu.make_async_copy(w_ref.at[rows(i), lanes], held.at[slot], sems.at[slot])

    slots = min(held.shape[0], blocks)
    for i in range(slots):
        copy(i, i).start()

    def one(i, carry):
        slot = lax.rem(i, slots)
        copy(i, slot).wait()
        use(at(i), held[slot])

        @pl.when(i + slots < blocks)
        def _():
            copy(i + slots, slot).start()

        return carry

    lax.fori_loop(0, blocks, one, 0)


def call(kernel, weights, others, outs, scratch, count, size, n_lanes, out, name, limit):
    n_in, n_out, n_scratch = len(others), len(outs), len(scratch)

    def whole(*refs):
        ins, rest = refs[1 : 1 + n_in], refs[1 + n_in :]
        held, sems = rest[n_out + n_scratch :]
        kernel(refs[0], ins, rest[:n_out], rest[n_out : n_out + n_scratch], held, sems)

    slots = max(2, min(count // size, IN_FLIGHT // (4 * size * n_lanes)))
    scratch = list(scratch) + [pltpu.VMEM((slots, size, n_lanes), f32), pltpu.SemaphoreType.DMA((slots,))]
    return pl.pallas_call(
        whole,
        in_specs=[FAR] + [WHOLE] * n_in,
        out_specs=[WHOLE] * n_out,
        out_shape=[jax.ShapeDtypeStruct(shape, f32) for shape in outs],
        scratch_shapes=scratch,
        compiler_params=pltpu.CompilerParams(vmem_limit_bytes=limit),
        cost_estimate=pl.CostEstimate(
            flops=6 * out * count * n_lanes, bytes_accessed=4 * count * n_lanes, transcendentals=0
        ),
        name=name,
    )(weights, *others)


def down(weights, pieces, places, out, first, count, lanes, name, chunks=0, before=None, squares=None, limit=VMEM_LIMIT):
    size = block_of(count, 512)
    n_lanes = lanes.stop - lanes.start
    n_pieces = len(pieces)
    share = out // chunks if chunks else out
    gives = isinstance(squares, str)
    takes = squares is not None and not gives
    extra = 128 if takes else 0
    others = list(pieces) + ([before] if before is not None else []) + ([squares] if takes else [])
    outs = [(share, n_lanes + extra)] * (chunks or 1) + ([(8, 128)] if gives else [])

    def kernel(w_ref, ins, out_refs, scratch, held, sems):
        full, parts, total = scratch

        def use(at, block):
            x = parts[:, at]
            high, low = split(block)
            both = dot(x, high, NN)
            total[...] += both[:out] + both[out:] + dot(x[:out], low, NN)

        total[...] = jnp.zeros_like(total) if before is None else ins[n_pieces][...]
        stage(ins[:n_pieces], places, full, parts)
        stream(w_ref, held, sems, first, count, size, lanes, use)
        if not chunks:
            out_refs[0][...] = total[...]
        for k in range(chunks):
            at = rows_at((lax.axis_index("rows") ^ k) * share, share)
            out_refs[k][:, 0:n_lanes] = total[at, :]
        if gives:
            out_refs[-1][...] = jnp.full((8, 128), jnp.sum(full[...] * full[...]), f32)
        if takes:
            sum_sq = jnp.sum(full[...] * full[...]) + jnp.max(ins[-1][0:1, :])
            for k in range(chunks):
                out_refs[k][:, n_lanes : n_lanes + extra] = jnp.full((share, extra), sum_sq, f32)

    scratch = [pltpu.VMEM((out, count), f32), pltpu.VMEM((2 * out, count), bf16), pltpu.VMEM((out, n_lanes), f32)]
    return call(kernel, weights, others, outs, scratch, count, size, n_lanes, out, name, limit)


def across(weights, pieces, places, out, first, count, lanes, name, before=None, halves=False, limit=VMEM_LIMIT):
    width = lanes.stop - lanes.start
    size = block_of(count, 512)
    half = out // 2
    n_pieces = len(pieces)
    outs = [(half, count)] * 2 if halves else [(out, count)]
    others = list(pieces) + ([before] if before is not None else [])

    def kernel(w_ref, ins, out_refs, scratch, held, sems):
        full, parts = scratch[:2]
        total = scratch[2] if halves else out_refs[0]

        def use(at, block):
            high, low = split(block)
            both = dot(parts[...], high, NT)
            sums = both[:out] + both[out:] + dot(parts[0:out], low, NT)
            if before is not None:
                sums = sums + ins[n_pieces][:, pl.ds(pl.multiple_of(offset(first, size) + at.start, size), size)]
            total[:, at] = sums

        stage(ins[:n_pieces], places, full, parts)
        stream(w_ref, held, sems, first, count, size, lanes, use)
        if halves:
            core = core_of()
            out_refs[0][...] = total[rows_at((1 - core) * half, half), :]
            out_refs[1][...] = total[rows_at(core * half, half), :]

    scratch = [pltpu.VMEM((out, width), f32), pltpu.VMEM((2 * out, width), bf16)]
    scratch += [pltpu.VMEM((out, count), f32)] if halves else []
    return call(kernel, weights, others, outs, scratch, count, size, width, out, name, limit)


def tile_and_logits(features, centers, coeffs):
    rows, width = features.shape
    count = centers.shape[0]
    out = coeffs.shape[0]
    half = out // 2
    size = block_of(rows, 512)
    gain = 2.0 * LOG2E / width

    def kernel(x_ref, c_ref, a_ref, tile_ref, theirs, mine, wide, norms, parts, total):
        @pl.when(pl.program_id(0) == 0)
        def _():
            c = c_ref[...]
            high, mid, low = split3(c * (2.0 * gain))
            wide[...] = jnp.concatenate([high, high, mid, mid, low, high], axis=1)
            norms[...] = lax.dot_general(
                jnp.full((8, width), gain, f32),
                c * c,
                NT,
                precision=lax.Precision.HIGHEST,
                preferred_element_type=f32,
            )
            high, low = split(a_ref[...])
            parts[0:out] = high
            parts[out : 2 * out] = low

        x = x_ref[...]
        high, mid, low = split3(x)
        cross = dot(jnp.concatenate([high, mid, high, mid, high, low], axis=1), wide[...], NT)
        norm = jnp.sum(x * x, axis=1, keepdims=True) * gain
        tile = jnp.exp2((cross - norm) - norms[0:1, :])
        tile_ref[...] = tile
        high, low = split(tile)
        both = dot(parts[...], high, NT)
        total[...] = both[:out] + both[out:] + dot(parts[0:out], low, NT)
        core = core_of()
        theirs[...] = total[rows_at((1 - core) * half, half), :]
        mine[...] = total[rows_at(core * half, half), :]

    return pl.pallas_call(
        kernel,
        grid=(rows // size,),
        in_specs=[
            pl.BlockSpec((size, width), lambda i: (i, 0)),
            pl.BlockSpec((count, width), lambda i: (0, 0)),
            pl.BlockSpec((out, count), lambda i: (0, 0)),
        ],
        out_specs=[
            pl.BlockSpec((size, count), lambda i: (i, 0)),
            pl.BlockSpec((half, size), lambda i: (0, i)),
            pl.BlockSpec((half, size), lambda i: (0, i)),
        ],
        out_shape=[
            jax.ShapeDtypeStruct((rows, count), f32),
            jax.ShapeDtypeStruct((half, rows), f32),
            jax.ShapeDtypeStruct((half, rows), f32),
        ],
        scratch_shapes=[
            pltpu.VMEM((count, 6 * width), bf16),
            pltpu.VMEM((8, count), f32),
            pltpu.VMEM((2 * out, count), bf16),
            pltpu.VMEM((out, size), f32),
        ],
        compiler_params=pltpu.CompilerParams(vmem_limit_bytes=TILE_LIMIT),
        cost_estimate=pl.CostEstimate(
            flops=12 * rows * width * count, bytes_accessed=4 * rows * count, transcendentals=rows * count
        ),
        name="tile_and_logits",
    )(features, centers, coeffs)


def add_and_cut(first, second, chips, name):
    rows, count = first.shape
    share = rows // chips

    def kernel(a_ref, b_ref, *outs):
        chip = chip_of()
        for k in range(chips):
            at = rows_at((chip ^ k) * share, share)
            outs[k][...] = a_ref[at, :] + b_ref[at, :]

    return pl.pallas_call(
        kernel,
        in_specs=[WHOLE] * 2,
        out_specs=[WHOLE] * chips,
        out_shape=[jax.ShapeDtypeStruct((share, count), f32)] * chips,
        compiler_params=pltpu.CompilerParams(vmem_limit_bytes=SMALL_LIMIT),
        name=name,
    )(first, second)


def update(cuts, a, elements, scale=None):
    rows, count = a.shape
    n_cuts = len(cuts)

    def kernel(*refs):
        back = refs[0][...]
        for ref in refs[1:n_cuts]:
            back = back + ref[...]
        if scale is None:
            step = step_size / jnp.sqrt(back[0:8, count:] / elements + epsilon)
            refs[-1][...] = step
        else:
            step = refs[n_cuts + 1][...]
        refs[n_cuts + (1 if scale is None else 2)][...] = refs[n_cuts][...] - step[0:1, 0:1] * back[:, 0:count]

    return pl.pallas_call(
        kernel,
        in_specs=[WHOLE] * (n_cuts + (1 if scale is None else 2)),
        out_specs=[WHOLE] * (2 if scale is None else 1),
        out_shape=[jax.ShapeDtypeStruct((rows, count), f32)] + ([jax.ShapeDtypeStruct((8, 128), f32)] if scale is None else []),
        compiler_params=pltpu.CompilerParams(vmem_limit_bytes=SMALL_LIMIT),
        name="update",
    )(*cuts, a, *([] if scale is None else [scale]))


def assemble(pieces, places, shape, name):
    n_pieces = len(pieces)

    def kernel(*refs):
        for piece, (start, lanes) in zip(refs[:n_pieces], places()):
            refs[n_pieces][rows_at(start, piece.shape[0]), lanes] = piece[...]

    return pl.pallas_call(
        kernel,
        in_specs=[WHOLE] * n_pieces,
        out_specs=WHOLE,
        out_shape=jax.ShapeDtypeStruct(shape, f32),
        compiler_params=pltpu.CompilerParams(vmem_limit_bytes=SMALL_LIMIT),
        name=name,
    )(*pieces)


def swap(x, axis, mask):
    size = lax.axis_size(axis)
    return lax.ppermute(x, axis, [(i, i ^ mask) for i in range(size)])


def body(features, centers, labels, coeffs, precond):
    depth_ranks = lax.axis_size("rows")
    chips = lax.axis_size("centers") // 2
    rows_here = features.shape[0]
    rows_total = rows_here * depth_ranks
    count, out = coeffs.shape
    center_total = count * lax.axis_size("centers")
    half = out // 2
    share = out // depth_ranks
    part = out // chips
    cols = count // 2
    row_half = precond.shape[0] // 2
    p_rows = precond.shape[0]
    left, right = slice(0, cols), slice(cols, count)
    every = slice(None)

    rank = lax.axis_index("rows")
    core = core_of()
    targets = lax.dynamic_slice_in_dim(labels.T, core * half, half, 0).astype(f32)
    a = coeffs.T
    a_share = lax.dynamic_slice_in_dim(a, rank * share, share, 0)
    a_halves = [a_share[:, left], a_share[:, right]]

    def core_places():
        me = core_of()
        return [(me * half, every), ((1 - me) * half, every)]

    def rank_places():
        return [((lax.axis_index("rows") ^ k) * share, every) for k in range(depth_ranks)]

    def rank_places_both():
        return [(at, lanes) for lanes in (left, right) for at, _ in rank_places()]

    def chip_places():
        return [((chip_of() ^ k) * part, every) for k in range(chips)]

    def chip_places_both():
        me = core_of()
        lanes = [pl.ds(pl.multiple_of(who * row_half, row_half), row_half) for who in (me, 1 - me)]
        return [(at, both) for both in lanes for at, _ in chip_places()]

    def my_rows():
        return core_of() * row_half

    def other_rows():
        return (1 - core_of()) * row_half

    def to_rank(cuts):
        return [cuts[0]] + [swap(cuts[k], "rows", k) for k in range(1, depth_ranks)]

    def sum_of(cuts):
        total = cuts[0]
        for cut in cuts[1:]:
            total = total + cut
        return total

    def all_rows(x):
        return [x] + [swap(x, "rows", k) for k in range(1, depth_ranks)]

    a_pieces = None
    for step in range(STEPS):
        if step == 0:
            tile, theirs, mine = tile_and_logits(features, centers, a)
        else:
            theirs, mine = across(
                tile, a_pieces, rank_places_both, out, 0, rows_here, slice(0, count), "logits", halves=True, limit=NEAR_LIMIT
            )
        logits = mine + swap(theirs, "centers", 1)
        full = logits
        for k in range(1, chips):
            full = full + swap(logits, "centers", 2 * k)
        resid = (jax.nn.sigmoid(full) - targets) / rows_total
        resids = [resid, swap(resid, "centers", 1)]
        grads = []
        for lanes, name in ((left, "grada"), (right, "gradb")):
            cuts = down(tile, resids, core_places, out, 0, rows_here, lanes, name, chunks=depth_ranks, limit=NEAR_LIMIT)
            grads.append(all_rows(sum_of(to_rank(cuts))))
        (begun,) = across(precond, grads[0], rank_places, out, 0, p_rows, left, "fwda")
        (theirs,) = across(precond, grads[1], rank_places, out, other_rows, row_half, right, "fwdb", before=begun)
        (mine,) = across(precond, grads[1], rank_places, out, my_rows, row_half, right, "fwdc", before=begun)
        cuts = add_and_cut(mine, swap(theirs, "centers", 1), chips, "cut")
        fwd = cuts[0]
        for k in range(1, chips):
            fwd = fwd + swap(cuts[k], "centers", 2 * k)
        fwds = [fwd] + [swap(fwd, "centers", 2 * k) for k in range(1, chips)]
        others = swap(jnp.concatenate(fwds, axis=0), "centers", 1)
        others = [others[k * part : (k + 1) * part] for k in range(chips)]
        begun, squares = down(precond, fwds, chip_places, out, my_rows, row_half, left, "backa", squares="sum")
        cuts = down(
            precond,
            others,
            chip_places,
            out,
            other_rows,
            row_half,
            left,
            "backb",
            chunks=depth_ranks,
            before=begun,
            squares=squares,
        )
        first, scale = update(to_rank(cuts), a_halves[0], center_total * out)
        cuts = down(
            precond, fwds + others, chip_places_both, out, 0, p_rows, right, "backc", chunks=depth_ranks
        )
        (second,) = update(to_rank(cuts), a_halves[1], center_total * out, scale)
        a_halves = [first, second]
        a_pieces = all_rows(first) + all_rows(second)
    return assemble(a_pieces, rank_places_both, (out, count), "result").T


def plain_tile(rows_x, centers_x):
    width = rows_x.shape[1]
    left = jnp.sum(rows_x * rows_x, axis=1)
    right = jnp.sum(centers_x * centers_x, axis=1)
    cross = jnp.dot(rows_x, centers_x.T, precision=lax.Precision.HIGHEST)
    return jnp.exp(-2.0 * (left[:, None] + right[None, :] - 2.0 * cross) / width)


def plain_body(features, centers, labels, coeffs, precond):
    rows_total = features.shape[0] * lax.axis_size("rows")
    center_total = coeffs.shape[0] * lax.axis_size("centers")
    targets = labels.astype(f32)
    share_rows = features.shape[0] // lax.axis_size("centers")
    highest = lax.Precision.HIGHEST
    tile = plain_tile(features, centers)
    for step in range(STEPS):
        part = jnp.dot(tile, coeffs, precision=highest)
        share = lax.psum_scatter(part, "centers", scatter_dimension=0, tiled=True)
        offset = lax.axis_index("centers") * share_rows
        share_y = lax.dynamic_slice_in_dim(targets, offset, share_rows, 0)
        share_resid = (jax.nn.sigmoid(share) - share_y) / rows_total
        resid = lax.all_gather(share_resid, "centers", axis=0, tiled=True)
        grad = lax.psum(lax.dot_general(tile, resid, (((0,), (0,)), ((), ())), precision=highest), "rows")
        fwd = lax.psum(jnp.dot(precond, grad, precision=highest), "centers")
        back = lax.psum(lax.dot_general(precond, fwd, (((0,), (0,)), ((), ())), precision=highest), "rows")
        total = lax.psum(jnp.sum(fwd * fwd), "rows")
        scale = step_size / jnp.sqrt(total / (center_total * fwd.shape[1]) + epsilon)
        coeffs = coeffs - scale * back
    return coeffs


def fits(ranks, cols, features, coeffs, precond):
    if cols % 2 or ranks & (ranks - 1) or cols & (cols - 1):
        return False
    out = coeffs.shape[1]
    lanes = (features.shape[0] // ranks, coeffs.shape[0] // cols // 2, precond.shape[0] // ranks // 2)
    return out % (8 * ranks) == 0 and out % (4 * cols) == 0 and out % 16 == 0 and all(n % 128 == 0 for n in lanes)


def solution(mesh):
    in_specs = (
        P("rows", None),
        P("centers", None),
        P("rows", None),
        P("centers", None),
        P("rows", "centers"),
    )
    out_specs = P("centers", None)

    def program(features, centers, labels, coeffs, precond):
        fit = fits(mesh.shape["rows"], mesh.shape["centers"], features, coeffs, precond)
        one = jax.shard_map(
            body if fit else plain_body, mesh=mesh, in_specs=in_specs, out_specs=out_specs, check_vma=False
        )
        return one(features, centers, labels, coeffs, precond)

    return program
```

```python
import functools

import jax
import jax.numpy as jnp
from jax import lax
from jax.experimental import pallas as pl
from jax.experimental.pallas import tpu as pltpu
from jax.sharding import PartitionSpec as P

STEPS = 2
step_size = 0.5
epsilon = 1e-06

f32 = jnp.float32
bf16 = jnp.bfloat16
LOG2E = 1.4426950408889634
NN = (((1,), (0,)), ((), ()))
NT = (((1,), (1,)), ((), ()))
WHOLE = pl.BlockSpec(memory_space=pltpu.VMEM)
FAR = pl.BlockSpec(memory_space=pltpu.HBM)
VMEM_LIMIT = 13 << 20
TILE_LIMIT = 30 << 20
NEAR_LIMIT = 13 << 20
SMALL_LIMIT = 6 << 20
IN_FLIGHT = 6 << 20


def dot(a, b, dims):
    return lax.dot_general(a, b, dims, preferred_element_type=f32)


def split(x):
    high = x.astype(bf16)
    return high, (x - high.astype(f32)).astype(bf16)


def split3(x):
    high = x.astype(bf16)
    rest = x - high.astype(f32)
    mid = rest.astype(bf16)
    return high, mid, (rest - mid.astype(f32)).astype(bf16)


def core_of():
    return lax.rem(lax.axis_index("centers"), 2)


def chip_of():
    return lax.div(lax.axis_index("centers"), 2)


def rows_at(start, count):
    if isinstance(start, int):
        return pl.ds(start, count)
    return pl.ds(pl.multiple_of(start, count), count)


def stage(pieces, places, full, parts):
    for piece, (start, lanes) in zip(pieces, places()):
        full[rows_at(start, piece.shape[0]), lanes] = piece[...]
    high, low = split(full[...])
    out = full.shape[0]
    parts[0:out] = high
    parts[out : 2 * out] = low


def block_of(total, most):
    size = min(total, most)
    while total % size:
        size //= 2
    return size


def offset(first, size):
    return first if isinstance(first, int) else pl.multiple_of(first(), size)


def stream(w_ref, held, sems, first, count, size, lanes, use):
    blocks = count // size
    start = offset(first, size)

    def at(i):
        return pl.ds(pl.multiple_of(i * size, size), size)

    def rows(i):
        return pl.ds(pl.multiple_of(start + i * size, size), size)

    def copy(i, slot):
        return pltpu.make_async_copy(w_ref.at[rows(i), lanes], held.at[slot], sems.at[slot])

    slots = min(held.shape[0], blocks)
    for i in range(slots):
        copy(i, i).start()

    def one(i, carry):
        slot = lax.rem(i, slots)
        copy(i, slot).wait()
        use(at(i), held[slot])

        @pl.when(i + slots < blocks)
        def _():
            copy(i + slots, slot).start()

        return carry

    lax.fori_loop(0, blocks, one, 0)


def stream_near(sources, size, use):
    for ref, first, count, at in sources:

        def one(i, carry, ref=ref, first=first, at=at):
            use(pl.ds(pl.multiple_of(at + i * size, size), size), ref[first + i])
            return carry

        lax.fori_loop(0, count, one, 0)


def call(kernel, weights, others, outs, scratch, count, size, n_lanes, out, name, limit, near=False, keep=False):
    weights = list(weights) if near else [weights]
    n_weights, n_in, n_out, n_scratch = len(weights), len(others), len(outs), len(scratch)

    def whole(*refs):
        ins, rest = refs[n_weights : n_weights + n_in], refs[n_weights + n_in :]
        if near:
            held = sems = None
        elif keep:
            held, sems = rest[n_out], rest[-1]
        else:
            held, sems = rest[n_out + n_scratch :]
        first = n_out + (1 if keep else 0)
        kernel(refs[:n_weights], ins, rest[:n_out], rest[first : first + n_scratch], held, sems)

    slots = max(2, min(count // size, IN_FLIGHT // (4 * size * n_lanes)))
    scratch = list(scratch)
    outs = list(outs)
    if keep:
        slots = count // size
        outs.append((slots, size, n_lanes))
    elif not near:
        scratch.append(pltpu.VMEM((slots, size, n_lanes), f32))
    if not near:
        scratch.append(pltpu.SemaphoreType.DMA((slots,)))
    return pl.pallas_call(
        whole,
        in_specs=[WHOLE if near else FAR] * n_weights + [WHOLE] * n_in,
        out_specs=[WHOLE] * len(outs),
        out_shape=[jax.ShapeDtypeStruct(shape, f32) for shape in outs],
        scratch_shapes=scratch,
        compiler_params=pltpu.CompilerParams(vmem_limit_bytes=limit),
        cost_estimate=pl.CostEstimate(
            flops=6 * out * count * n_lanes, bytes_accessed=4 * count * n_lanes, transcendentals=0
        ),
        name=name,
    )(*weights, *others)


def down(weights, pieces, places, out, first, count, lanes, name, chunks=0, before=None, squares=None, limit=VMEM_LIMIT, near=None):
    size = block_of(count, 512)
    n_lanes = lanes.stop - lanes.start
    n_pieces = len(pieces)
    share = out // chunks if chunks else out
    gives = isinstance(squares, str)
    takes = squares is not None and not gives
    extra = 128 if takes else 0
    others = list(pieces) + ([before] if before is not None else []) + ([squares] if takes else [])
    outs = [(share, n_lanes + extra)] * (chunks or 1) + ([(8, 128)] if gives else [])

    def kernel(w_ref, ins, out_refs, scratch, held, sems):
        full, parts, total = scratch

        def use(at, block):
            x = parts[:, at]
            high, low = split(block)
            both = dot(x, high, NN)
            total[...] += both[:out] + both[out:] + dot(x[:out], low, NN)

        total[...] = jnp.zeros_like(total) if before is None else ins[n_pieces][...]
        stage(ins[:n_pieces], places, full, parts)
        if near is None:
            stream(w_ref[0], held, sems, first, count, size, lanes, use)
        else:
            stream_near([(ref, *rest) for ref, rest in zip(w_ref, near(size))], size, use)
        if not chunks:
            out_refs[0][...] = total[...]
        for k in range(chunks):
            at = rows_at((lax.axis_index("rows") ^ k) * share, share)
            out_refs[k][:, 0:n_lanes] = total[at, :]
        if gives:
            out_refs[-1][...] = jnp.full((8, 128), jnp.sum(full[...] * full[...]), f32)
        if takes:
            sum_sq = jnp.sum(full[...] * full[...]) + jnp.max(ins[-1][0:1, :])
            for k in range(chunks):
                out_refs[k][:, n_lanes : n_lanes + extra] = jnp.full((share, extra), sum_sq, f32)

    scratch = [pltpu.VMEM((out, count), f32), pltpu.VMEM((2 * out, count), bf16), pltpu.VMEM((out, n_lanes), f32)]
    return call(kernel, weights, others, outs, scratch, count, size, n_lanes, out, name, limit, near is not None)


def across(weights, pieces, places, out, first, count, lanes, name, before=None, halves=False, limit=VMEM_LIMIT, near=False, keep=False):
    width = lanes.stop - lanes.start
    size = block_of(count, 512)
    weights = [weights] if near else weights
    half = out // 2
    n_pieces = len(pieces)
    outs = [(half, count)] * 2 if halves else [(out, count)]
    others = list(pieces) + ([before] if before is not None else [])

    def kernel(w_ref, ins, out_refs, scratch, held, sems):
        full, parts = scratch[:2]
        total = scratch[2] if halves else out_refs[0]

        def use(at, block):
            high, low = split(block)
            both = dot(parts[...], high, NT)
            sums = both[:out] + both[out:] + dot(parts[0:out], low, NT)
            if before is not None:
                sums = sums + ins[n_pieces][:, pl.ds(pl.multiple_of(offset(first, size) + at.start, size), size)]
            total[:, at] = sums

        stage(ins[:n_pieces], places, full, parts)
        if near:
            stream_near([(w_ref[0], 0, count // size, 0)], size, use)
        else:
            stream(w_ref[0], held, sems, first, count, size, lanes, use)
        if halves:
            core = core_of()
            out_refs[0][...] = total[rows_at((1 - core) * half, half), :]
            out_refs[1][...] = total[rows_at(core * half, half), :]

    scratch = [pltpu.VMEM((out, width), f32), pltpu.VMEM((2 * out, width), bf16)]
    scratch += [pltpu.VMEM((out, count), f32)] if halves else []
    return call(kernel, weights, others, outs, scratch, count, size, width, out, name, limit, near, keep)


def tile_and_logits(features, centers, coeffs):
    rows, width = features.shape
    count = centers.shape[0]
    out = coeffs.shape[0]
    half = out // 2
    size = block_of(rows, 512)
    gain = 2.0 * LOG2E / width

    def kernel(x_ref, c_ref, a_ref, tile_ref, theirs, mine, wide, norms, parts, total):
        @pl.when(pl.program_id(0) == 0)
        def _():
            c = c_ref[...]
            high, mid, low = split3(c * (2.0 * gain))
            wide[...] = jnp.concatenate([high, high, mid, mid, low, high], axis=1)
            norms[...] = lax.dot_general(
                jnp.full((8, width), gain, f32),
                c * c,
                NT,
                precision=lax.Precision.HIGHEST,
                preferred_element_type=f32,
            )
            high, low = split(a_ref[...])
            parts[0:out] = high
            parts[out : 2 * out] = low

        x = x_ref[...]
        high, mid, low = split3(x)
        cross = dot(jnp.concatenate([high, mid, high, mid, high, low], axis=1), wide[...], NT)
        norm = jnp.sum(x * x, axis=1, keepdims=True) * gain
        tile = jnp.exp2((cross - norm) - norms[0:1, :])
        tile_ref[...] = tile
        high, low = split(tile)
        both = dot(parts[...], high, NT)
        total[...] = both[:out] + both[out:] + dot(parts[0:out], low, NT)
        core = core_of()
        theirs[...] = total[rows_at((1 - core) * half, half), :]
        mine[...] = total[rows_at(core * half, half), :]

    return pl.pallas_call(
        kernel,
        grid=(rows // size,),
        in_specs=[
            pl.BlockSpec((size, width), lambda i: (i, 0)),
            pl.BlockSpec((count, width), lambda i: (0, 0)),
            pl.BlockSpec((out, count), lambda i: (0, 0)),
        ],
        out_specs=[
            pl.BlockSpec((size, count), lambda i: (i, 0)),
            pl.BlockSpec((half, size), lambda i: (0, i)),
            pl.BlockSpec((half, size), lambda i: (0, i)),
        ],
        out_shape=[
            jax.ShapeDtypeStruct((rows, count), f32),
            jax.ShapeDtypeStruct((half, rows), f32),
            jax.ShapeDtypeStruct((half, rows), f32),
        ],
        scratch_shapes=[
            pltpu.VMEM((count, 6 * width), bf16),
            pltpu.VMEM((8, count), f32),
            pltpu.VMEM((2 * out, count), bf16),
            pltpu.VMEM((out, size), f32),
        ],
        compiler_params=pltpu.CompilerParams(vmem_limit_bytes=TILE_LIMIT),
        cost_estimate=pl.CostEstimate(
            flops=12 * rows * width * count, bytes_accessed=4 * rows * count, transcendentals=rows * count
        ),
        name="tile_and_logits",
    )(features, centers, coeffs)


def add_and_cut(first, second, chips, name):
    rows, count = first.shape
    share = rows // chips

    def kernel(a_ref, b_ref, *outs):
        chip = chip_of()
        for k in range(chips):
            at = rows_at((chip ^ k) * share, share)
            outs[k][...] = a_ref[at, :] + b_ref[at, :]

    return pl.pallas_call(
        kernel,
        in_specs=[WHOLE] * 2,
        out_specs=[WHOLE] * chips,
        out_shape=[jax.ShapeDtypeStruct((share, count), f32)] * chips,
        compiler_params=pltpu.CompilerParams(vmem_limit_bytes=SMALL_LIMIT),
        name=name,
    )(first, second)


def small(kernel, others, outs, name):
    return pl.pallas_call(
        kernel,
        in_specs=[WHOLE] * len(others),
        out_specs=[WHOLE] * len(outs),
        out_shape=[jax.ShapeDtypeStruct(shape, f32) for shape in outs],
        compiler_params=pltpu.CompilerParams(vmem_limit_bytes=SMALL_LIMIT),
        name=name,
    )(*others)


def add_up(terms, name):
    def kernel(*refs):
        total = refs[0][...]
        for ref in refs[1:-1]:
            total = total + ref[...]
        refs[-1][...] = total

    return small(kernel, terms, [terms[0].shape], name)[0]


def residuals(logits, labels, rows_total):
    half = logits[0].shape[0]

    def kernel(*refs):
        total = refs[0][...]
        for ref in refs[1:-2]:
            total = total + ref[...]
        targets = refs[-2][rows_at(core_of() * half, half), :].astype(f32)
        refs[-1][...] = (jax.nn.sigmoid(total) - targets) / rows_total

    return small(kernel, [*logits, labels], [logits[0].shape], "resid")[0]


def rank_share(a, share, lanes):
    def kernel(a_ref, *outs):
        at = rows_at(lax.axis_index("rows") * share, share)
        for out, cut in zip(outs, lanes):
            out[...] = a_ref[at, cut]

    return small(kernel, [a], [(share, cut.stop - cut.start) for cut in lanes], "share")


def update(cuts, a, elements, scale=None):
    rows, count = a.shape
    n_cuts = len(cuts)

    def kernel(*refs):
        back = refs[0][...]
        for ref in refs[1:n_cuts]:
            back = back + ref[...]
        if scale is None:
            step = step_size / jnp.sqrt(back[0:8, count:] / elements + epsilon)
            refs[-1][...] = step
        else:
            step = refs[n_cuts + 1][...]
        refs[n_cuts + (1 if scale is None else 2)][...] = refs[n_cuts][...] - step[0:1, 0:1] * back[:, 0:count]

    return pl.pallas_call(
        kernel,
        in_specs=[WHOLE] * (n_cuts + (1 if scale is None else 2)),
        out_specs=[WHOLE] * (2 if scale is None else 1),
        out_shape=[jax.ShapeDtypeStruct((rows, count), f32)] + ([jax.ShapeDtypeStruct((8, 128), f32)] if scale is None else []),
        compiler_params=pltpu.CompilerParams(vmem_limit_bytes=SMALL_LIMIT),
        name="update",
    )(*cuts, a, *([] if scale is None else [scale]))


def assemble(pieces, places, shape, name):
    n_pieces = len(pieces)

    def kernel(*refs):
        for piece, (start, lanes) in zip(refs[:n_pieces], places()):
            refs[n_pieces][rows_at(start, piece.shape[0]), lanes] = piece[...]

    return pl.pallas_call(
        kernel,
        in_specs=[WHOLE] * n_pieces,
        out_specs=WHOLE,
        out_shape=jax.ShapeDtypeStruct(shape, f32),
        compiler_params=pltpu.CompilerParams(vmem_limit_bytes=SMALL_LIMIT),
        name=name,
    )(*pieces)


def swap(x, axis, mask):
    size = lax.axis_size(axis)
    return lax.ppermute(x, axis, [(i, i ^ mask) for i in range(size)])


def body(features, centers, labels, coeffs, precond):
    depth_ranks = lax.axis_size("rows")
    chips = lax.axis_size("centers") // 2
    rows_here = features.shape[0]
    rows_total = rows_here * depth_ranks
    count, out = coeffs.shape
    center_total = count * lax.axis_size("centers")
    half = out // 2
    share = out // depth_ranks
    part = out // chips
    cols = count // 2
    row_half = precond.shape[0] // 2
    p_rows = precond.shape[0]
    left, right = slice(0, cols), slice(cols, count)
    every = slice(None)

    a = coeffs.T
    a_halves = rank_share(a, share, (left, right))

    def core_places():
        me = core_of()
        return [(me * half, every), ((1 - me) * half, every)]

    def rank_places():
        return [((lax.axis_index("rows") ^ k) * share, every) for k in range(depth_ranks)]

    def rank_places_both():
        return [(at, lanes) for lanes in (left, right) for at, _ in rank_places()]

    def chip_places():
        return [((chip_of() ^ k) * part, every) for k in range(chips)]

    def chip_places_both():
        me = core_of()
        own, other = [pl.ds(pl.multiple_of(who * row_half, row_half), row_half) for who in (me, 1 - me)]
        return [(at, own) for at, _ in chip_places()] + [(0, other)]

    def whole_place():
        return [(0, every)]

    def my_rows():
        return core_of() * row_half

    def other_rows():
        return (1 - core_of()) * row_half

    def to_rank(cuts):
        return [cuts[0]] + [swap(cuts[k], "rows", k) for k in range(1, depth_ranks)]

    def all_rows(x):
        return [x] + [swap(x, "rows", k) for k in range(1, depth_ranks)]

    a_pieces = None
    for step in range(STEPS):
        if step == 0:
            tile, theirs, mine = tile_and_logits(features, centers, a)
        else:
            theirs, mine = across(
                tile, a_pieces, rank_places_both, out, 0, rows_here, slice(0, count), "logits", halves=True, limit=NEAR_LIMIT
            )
        logits = add_up([mine, swap(theirs, "centers", 1)], "chip_logits")
        logits = [logits] + [swap(logits, "centers", 2 * k) for k in range(1, chips)]
        resid = residuals(logits, labels.T, rows_total)
        resids = [resid, swap(resid, "centers", 1)]
        grads = []
        for lanes, name in ((left, "grada"), (right, "gradb")):
            cuts = down(tile, resids, core_places, out, 0, rows_here, lanes, name, chunks=depth_ranks, limit=NEAR_LIMIT)
            grads.append(all_rows(add_up(to_rank(cuts), "grad_sum")))
        places = rank_places
        if step == 0:
            begun, near_left = across(precond, grads[0], places, out, 0, p_rows, left, "fwda", keep=True)
            theirs, near_other = across(
                precond, grads[1], places, out, other_rows, row_half, right, "fwdb", before=begun, keep=True
            )
            mine, near_mine = across(
                precond, grads[1], places, out, my_rows, row_half, right, "fwdc", before=begun, keep=True
            )
        else:
            (begun,) = across(near_left, grads[0], places, out, 0, p_rows, left, "fwda", near=True)
            (theirs,) = across(
                near_other, grads[1], places, out, other_rows, row_half, right, "fwdb", before=begun, near=True
            )
            (mine,) = across(
                near_mine, grads[1], places, out, my_rows, row_half, right, "fwdc", before=begun, near=True
            )
        cuts = add_and_cut(mine, swap(theirs, "centers", 1), chips, "cut")
        fwd = add_up([cuts[0]] + [swap(cuts[k], "centers", 2 * k) for k in range(1, chips)], "fwd_sum")
        fwds = [fwd] + [swap(fwd, "centers", 2 * k) for k in range(1, chips)]
        others = [swap(assemble(fwds, chip_places, (out, row_half), "fwd_mine"), "centers", 1)]
        begun, squares = down(
            [near_left],
            fwds,
            chip_places,
            out,
            my_rows,
            row_half,
            left,
            "backa",
            squares="sum",
            near=lambda size: [(my_rows() // size, row_half // size, 0)],
        )
        cuts = down(
            [near_left],
            others,
            whole_place,
            out,
            other_rows,
            row_half,
            left,
            "backb",
            chunks=depth_ranks,
            before=begun,
            squares=squares,
            near=lambda size: [(other_rows() // size, row_half // size, 0)],
        )
        first, scale = update(to_rank(cuts), a_halves[0], center_total * out)
        cuts = down(
            [near_mine, near_other],
            fwds + others,
            chip_places_both,
            out,
            0,
            p_rows,
            right,
            "backc",
            chunks=depth_ranks,
            near=lambda size: [(0, row_half // size, my_rows()), (0, row_half // size, other_rows())],
        )
        (second,) = update(to_rank(cuts), a_halves[1], center_total * out, scale)
        a_halves = [first, second]
        a_pieces = all_rows(first) + all_rows(second)
    return assemble(a_pieces, rank_places_both, (out, count), "result").T


def plain_tile(rows_x, centers_x):
    width = rows_x.shape[1]
    left = jnp.sum(rows_x * rows_x, axis=1)
    right = jnp.sum(centers_x * centers_x, axis=1)
    cross = jnp.dot(rows_x, centers_x.T, precision=lax.Precision.HIGHEST)
    return jnp.exp(-2.0 * (left[:, None] + right[None, :] - 2.0 * cross) / width)


def plain_body(features, centers, labels, coeffs, precond):
    rows_total = features.shape[0] * lax.axis_size("rows")
    center_total = coeffs.shape[0] * lax.axis_size("centers")
    targets = labels.astype(f32)
    share_rows = features.shape[0] // lax.axis_size("centers")
    highest = lax.Precision.HIGHEST
    tile = plain_tile(features, centers)
    for step in range(STEPS):
        part = jnp.dot(tile, coeffs, precision=highest)
        share = lax.psum_scatter(part, "centers", scatter_dimension=0, tiled=True)
        offset = lax.axis_index("centers") * share_rows
        share_y = lax.dynamic_slice_in_dim(targets, offset, share_rows, 0)
        share_resid = (jax.nn.sigmoid(share) - share_y) / rows_total
        resid = lax.all_gather(share_resid, "centers", axis=0, tiled=True)
        grad = lax.psum(lax.dot_general(tile, resid, (((0,), (0,)), ((), ())), precision=highest), "rows")
        fwd = lax.psum(jnp.dot(precond, grad, precision=highest), "centers")
        back = lax.psum(lax.dot_general(precond, fwd, (((0,), (0,)), ((), ())), precision=highest), "rows")
        total = lax.psum(jnp.sum(fwd * fwd), "rows")
        scale = step_size / jnp.sqrt(total / (center_total * fwd.shape[1]) + epsilon)
        coeffs = coeffs - scale * back
    return coeffs


def fits(ranks, cols, features, coeffs, precond):
    if cols % 2 or ranks & (ranks - 1) or cols & (cols - 1):
        return False
    out = coeffs.shape[1]
    lanes = (features.shape[0] // ranks, coeffs.shape[0] // cols // 2, precond.shape[0] // ranks // 2)
    return out % (8 * ranks) == 0 and out % (4 * cols) == 0 and out % 16 == 0 and all(n % 128 == 0 for n in lanes)


def solution(mesh):
    in_specs = (
        P("rows", None),
        P("centers", None),
        P("rows", None),
        P("centers", None),
        P("rows", "centers"),
    )
    out_specs = P("centers", None)

    def program(features, centers, labels, coeffs, precond):
        fit = fits(mesh.shape["rows"], mesh.shape["centers"], features, coeffs, precond)
        one = jax.shard_map(
            body if fit else plain_body, mesh=mesh, in_specs=in_specs, out_specs=out_specs, check_vma=False
        )
        return one(features, centers, labels, coeffs, precond)

    return program
```

```python
import functools

import jax
import jax.numpy as jnp
from jax import lax
from jax.experimental import pallas as pl
from jax.experimental.pallas import tpu as pltpu
from jax.sharding import PartitionSpec as P

STEPS = 2
step_size = 0.5
epsilon = 1e-06

f32 = jnp.float32
bf16 = jnp.bfloat16
LOG2E = 1.4426950408889634
NN = (((1,), (0,)), ((), ()))
NT = (((1,), (1,)), ((), ()))
WHOLE = pl.BlockSpec(memory_space=pltpu.VMEM)
FAR = pl.BlockSpec(memory_space=pltpu.HBM)
VMEM_LIMIT = 13 << 20
TILE_LIMIT = 30 << 20
NEAR_LIMIT = 13 << 20
SMALL_LIMIT = 6 << 20
IN_FLIGHT = 6 << 20


def dot(a, b, dims):
    return lax.dot_general(a, b, dims, preferred_element_type=f32)


def split(x):
    high = x.astype(bf16)
    return high, (x - high.astype(f32)).astype(bf16)


def split3(x):
    high = x.astype(bf16)
    rest = x - high.astype(f32)
    mid = rest.astype(bf16)
    return high, mid, (rest - mid.astype(f32)).astype(bf16)


def core_of():
    return lax.rem(lax.axis_index("centers"), 2)


def chip_of():
    return lax.div(lax.axis_index("centers"), 2)


def rows_at(start, count):
    if isinstance(start, int):
        return pl.ds(start, count)
    return pl.ds(pl.multiple_of(start, count), count)


def stage(pieces, places, full, parts):
    for piece, (start, lanes) in zip(pieces, places()):
        full[rows_at(start, piece.shape[0]), lanes] = piece[...]
    high, low = split(full[...])
    out = full.shape[0]
    parts[0:out] = high
    parts[out : 2 * out] = low


def block_of(total, most):
    size = min(total, most)
    while total % size:
        size //= 2
    return size


def offset(first, size):
    return first if isinstance(first, int) else pl.multiple_of(first(), size)


def stream(w_ref, held, sems, first, count, size, lanes, use):
    blocks = count // size
    start = offset(first, size)

    def at(i):
        return pl.ds(pl.multiple_of(i * size, size), size)

    def rows(i):
        return pl.ds(pl.multiple_of(start + i * size, size), size)

    def copy(i, slot):
        return pltpu.make_async_copy(w_ref.at[rows(i), lanes], held.at[slot], sems.at[slot])

    slots = min(held.shape[0], blocks)
    for i in range(slots):
        copy(i, i).start()

    def one(i, carry):
        slot = lax.rem(i, slots)
        copy(i, slot).wait()
        use(at(i), held[slot])

        @pl.when(i + slots < blocks)
        def _():
            copy(i + slots, slot).start()

        return carry

    lax.fori_loop(0, blocks, one, 0)


def stream_near(sources, size, use):
    for ref, first, count, at, lanes in sources:

        def one(i, carry, ref=ref, first=first, at=at, lanes=lanes):
            use(pl.ds(pl.multiple_of(at + i * size, size), size), ref[first + i, :, lanes])
            return carry

        lax.fori_loop(0, count, one, 0)


def call(kernel, weights, others, outs, scratch, count, size, n_lanes, out, name, limit, near=False, keep=False):
    weights = list(weights) if near else [weights]
    n_weights, n_in, n_out, n_scratch = len(weights), len(others), len(outs), len(scratch)

    def whole(*refs):
        ins, rest = refs[n_weights : n_weights + n_in], refs[n_weights + n_in :]
        if near:
            held = sems = None
        elif keep:
            held, sems = rest[n_out], rest[-1]
        else:
            held, sems = rest[n_out + n_scratch :]
        first = n_out + (1 if keep else 0)
        kernel(refs[:n_weights], ins, rest[:n_out], rest[first : first + n_scratch], held, sems)

    slots = max(2, min(count // size, IN_FLIGHT // (4 * size * n_lanes)))
    scratch = list(scratch)
    outs = list(outs)
    if keep:
        slots = count // size
        outs.append((slots, size, n_lanes))
    elif not near:
        scratch.append(pltpu.VMEM((slots, size, n_lanes), f32))
    if not near:
        scratch.append(pltpu.SemaphoreType.DMA((slots,)))
    return pl.pallas_call(
        whole,
        in_specs=[WHOLE if near else FAR] * n_weights + [WHOLE] * n_in,
        out_specs=[WHOLE] * len(outs),
        out_shape=[jax.ShapeDtypeStruct(shape, f32) for shape in outs],
        scratch_shapes=scratch,
        compiler_params=pltpu.CompilerParams(vmem_limit_bytes=limit),
        cost_estimate=pl.CostEstimate(
            flops=6 * out * count * n_lanes, bytes_accessed=4 * count * n_lanes, transcendentals=0
        ),
        name=name,
    )(*weights, *others)


def down(weights, pieces, places, out, first, count, lanes, name, chunks=0, before=None, squares=None, limit=VMEM_LIMIT, near=None):
    size = block_of(count, 512)
    n_lanes = lanes.stop - lanes.start
    n_pieces = len(pieces)
    share = out // chunks if chunks else out
    gives = isinstance(squares, str)
    takes = squares is not None and not gives
    extra = 128 if takes else 0
    others = list(pieces) + ([before] if before is not None else []) + ([squares] if takes else [])
    outs = [(share, n_lanes + extra)] * (chunks or 1) + ([(8, 128)] if gives else [])

    def kernel(w_ref, ins, out_refs, scratch, held, sems):
        full, parts, total = scratch

        def use(at, block):
            x = parts[:, at]
            high, low = split(block)
            both = dot(x, high, NN)
            total[...] += both[:out] + both[out:] + dot(x[:out], low, NN)

        total[...] = jnp.zeros_like(total) if before is None else ins[n_pieces][...]
        stage(ins[:n_pieces], places, full, parts)
        if near is None:
            stream(w_ref[0], held, sems, first, count, size, lanes, use)
        else:
            stream_near([(ref, *rest) for ref, rest in zip(w_ref, near(size))], size, use)
        if not chunks:
            out_refs[0][...] = total[...]
        for k in range(chunks):
            at = rows_at((lax.axis_index("rows") ^ k) * share, share)
            out_refs[k][:, 0:n_lanes] = total[at, :]
        if gives:
            out_refs[-1][...] = jnp.full((8, 128), jnp.sum(full[...] * full[...]), f32)
        if takes:
            sum_sq = jnp.sum(full[...] * full[...]) + jnp.max(ins[-1][0:1, :])
            for k in range(chunks):
                out_refs[k][:, n_lanes : n_lanes + extra] = jnp.full((share, extra), sum_sq, f32)

    scratch = [pltpu.VMEM((out, count), f32), pltpu.VMEM((2 * out, count), bf16), pltpu.VMEM((out, n_lanes), f32)]
    return call(kernel, weights, others, outs, scratch, count, size, n_lanes, out, name, limit, near is not None)


def across(weights, pieces, places, out, first, count, lanes, name, before=None, halves=False, limit=VMEM_LIMIT, near=False, keep=False):
    width = lanes.stop - lanes.start
    size = block_of(count, 512)
    weights = [weights] if near else weights
    half = out // 2
    n_pieces = len(pieces)
    outs = [(half, count)] * 2 if halves else [(out, count)]
    others = list(pieces) + ([before] if before is not None else [])

    def kernel(w_ref, ins, out_refs, scratch, held, sems):
        full, parts = scratch[:2]
        total = scratch[2] if halves else out_refs[0]

        def use(at, block):
            high, low = split(block)
            both = dot(parts[...], high, NT)
            sums = both[:out] + both[out:] + dot(parts[0:out], low, NT)
            if before is not None:
                sums = sums + ins[n_pieces][:, pl.ds(pl.multiple_of(offset(first, size) + at.start, size), size)]
            total[:, at] = sums

        stage(ins[:n_pieces], places, full, parts)
        if near:
            stream_near([(w_ref[0], 0, count // size, 0, slice(None))], size, use)
        else:
            stream(w_ref[0], held, sems, first, count, size, lanes, use)
        if halves:
            core = core_of()
            out_refs[0][...] = total[rows_at((1 - core) * half, half), :]
            out_refs[1][...] = total[rows_at(core * half, half), :]

    scratch = [pltpu.VMEM((out, width), f32), pltpu.VMEM((2 * out, width), bf16)]
    scratch += [pltpu.VMEM((out, count), f32)] if halves else []
    return call(kernel, weights, others, outs, scratch, count, size, width, out, name, limit, near, keep)


def tile_and_logits(features, centers, coeffs):
    rows, width = features.shape
    count = centers.shape[0]
    out = coeffs.shape[0]
    half = out // 2
    size = block_of(rows, 512)
    gain = 2.0 * LOG2E / width

    def kernel(x_ref, c_ref, a_ref, tile_ref, theirs, mine, wide, norms, parts, total):
        @pl.when(pl.program_id(0) == 0)
        def _():
            c = c_ref[...]
            high, mid, low = split3(c * (2.0 * gain))
            wide[...] = jnp.concatenate([high, high, mid, mid, low, high], axis=1)
            norms[...] = lax.dot_general(
                jnp.full((8, width), gain, f32),
                c * c,
                NT,
                precision=lax.Precision.HIGHEST,
                preferred_element_type=f32,
            )
            high, low = split(a_ref[...])
            parts[0:out] = high
            parts[out : 2 * out] = low

        x = x_ref[...]
        high, mid, low = split3(x)
        cross = dot(jnp.concatenate([high, mid, high, mid, high, low], axis=1), wide[...], NT)
        norm = jnp.sum(x * x, axis=1, keepdims=True) * gain
        tile = jnp.exp2((cross - norm) - norms[0:1, :])
        tile_ref[0] = tile
        high, low = split(tile)
        both = dot(parts[...], high, NT)
        total[...] = both[:out] + both[out:] + dot(parts[0:out], low, NT)
        core = core_of()
        theirs[...] = total[rows_at((1 - core) * half, half), :]
        mine[...] = total[rows_at(core * half, half), :]

    return pl.pallas_call(
        kernel,
        grid=(rows // size,),
        in_specs=[
            pl.BlockSpec((size, width), lambda i: (i, 0)),
            pl.BlockSpec((count, width), lambda i: (0, 0)),
            pl.BlockSpec((out, count), lambda i: (0, 0)),
        ],
        out_specs=[
            pl.BlockSpec((1, size, count), lambda i: (i, 0, 0)),
            pl.BlockSpec((half, size), lambda i: (0, i)),
            pl.BlockSpec((half, size), lambda i: (0, i)),
        ],
        out_shape=[
            jax.ShapeDtypeStruct((rows // size, size, count), f32),
            jax.ShapeDtypeStruct((half, rows), f32),
            jax.ShapeDtypeStruct((half, rows), f32),
        ],
        scratch_shapes=[
            pltpu.VMEM((count, 6 * width), bf16),
            pltpu.VMEM((8, count), f32),
            pltpu.VMEM((2 * out, count), bf16),
            pltpu.VMEM((out, size), f32),
        ],
        compiler_params=pltpu.CompilerParams(vmem_limit_bytes=TILE_LIMIT),
        cost_estimate=pl.CostEstimate(
            flops=12 * rows * width * count, bytes_accessed=4 * rows * count, transcendentals=rows * count
        ),
        name="tile_and_logits",
    )(features, centers, coeffs)


def add_and_cut(first, second, chips, name):
    rows, count = first.shape
    share = rows // chips

    def kernel(a_ref, b_ref, *outs):
        chip = chip_of()
        for k in range(chips):
            at = rows_at((chip ^ k) * share, share)
            outs[k][...] = a_ref[at, :] + b_ref[at, :]

    return pl.pallas_call(
        kernel,
        in_specs=[WHOLE] * 2,
        out_specs=[WHOLE] * chips,
        out_shape=[jax.ShapeDtypeStruct((share, count), f32)] * chips,
        compiler_params=pltpu.CompilerParams(vmem_limit_bytes=SMALL_LIMIT),
        name=name,
    )(first, second)


def small(kernel, others, outs, name):
    return pl.pallas_call(
        kernel,
        in_specs=[WHOLE] * len(others),
        out_specs=[WHOLE] * len(outs),
        out_shape=[jax.ShapeDtypeStruct(shape, f32) for shape in outs],
        compiler_params=pltpu.CompilerParams(vmem_limit_bytes=SMALL_LIMIT),
        name=name,
    )(*others)


def add_up(terms, name):
    def kernel(*refs):
        total = refs[0][...]
        for ref in refs[1:-1]:
            total = total + ref[...]
        refs[-1][...] = total

    return small(kernel, terms, [terms[0].shape], name)[0]


def residuals(logits, labels, rows_total):
    half = logits[0].shape[0]

    def kernel(*refs):
        total = refs[0][...]
        for ref in refs[1:-2]:
            total = total + ref[...]
        targets = refs[-2][rows_at(core_of() * half, half), :].astype(f32)
        refs[-1][...] = (jax.nn.sigmoid(total) - targets) / rows_total

    return small(kernel, [*logits, labels], [logits[0].shape], "resid")[0]


def rank_share(a, share, lanes):
    def kernel(a_ref, *outs):
        at = rows_at(lax.axis_index("rows") * share, share)
        for out, cut in zip(outs, lanes):
            out[...] = a_ref[at, cut]

    return small(kernel, [a], [(share, cut.stop - cut.start) for cut in lanes], "share")


def update(cuts, a, elements, scale=None):
    rows, count = a.shape
    n_cuts = len(cuts)

    def kernel(*refs):
        back = refs[0][...]
        for ref in refs[1:n_cuts]:
            back = back + ref[...]
        if scale is None:
            step = step_size / jnp.sqrt(back[0:8, count:] / elements + epsilon)
            refs[-1][...] = step
        else:
            step = refs[n_cuts + 1][...]
        refs[n_cuts + (1 if scale is None else 2)][...] = refs[n_cuts][...] - step[0:1, 0:1] * back[:, 0:count]

    return pl.pallas_call(
        kernel,
        in_specs=[WHOLE] * (n_cuts + (1 if scale is None else 2)),
        out_specs=[WHOLE] * (2 if scale is None else 1),
        out_shape=[jax.ShapeDtypeStruct((rows, count), f32)] + ([jax.ShapeDtypeStruct((8, 128), f32)] if scale is None else []),
        compiler_params=pltpu.CompilerParams(vmem_limit_bytes=SMALL_LIMIT),
        name="update",
    )(*cuts, a, *([] if scale is None else [scale]))


def assemble(pieces, places, shape, name):
    n_pieces = len(pieces)

    def kernel(*refs):
        for piece, (start, lanes) in zip(refs[:n_pieces], places()):
            refs[n_pieces][rows_at(start, piece.shape[0]), lanes] = piece[...]

    return pl.pallas_call(
        kernel,
        in_specs=[WHOLE] * n_pieces,
        out_specs=WHOLE,
        out_shape=jax.ShapeDtypeStruct(shape, f32),
        compiler_params=pltpu.CompilerParams(vmem_limit_bytes=SMALL_LIMIT),
        name=name,
    )(*pieces)


def swap(x, axis, mask):
    size = lax.axis_size(axis)
    return lax.ppermute(x, axis, [(i, i ^ mask) for i in range(size)])


def body(features, centers, labels, coeffs, precond):
    depth_ranks = lax.axis_size("rows")
    chips = lax.axis_size("centers") // 2
    rows_here = features.shape[0]
    rows_total = rows_here * depth_ranks
    count, out = coeffs.shape
    center_total = count * lax.axis_size("centers")
    half = out // 2
    share = out // depth_ranks
    part = out // chips
    cols = count // 2
    row_half = precond.shape[0] // 2
    p_rows = precond.shape[0]
    left, right = slice(0, cols), slice(cols, count)
    every = slice(None)

    a = coeffs.T
    a_halves = rank_share(a, share, (left, right))

    def core_places():
        me = core_of()
        return [(me * half, every), ((1 - me) * half, every)]

    def rank_places():
        return [((lax.axis_index("rows") ^ k) * share, every) for k in range(depth_ranks)]

    def rank_places_both():
        return [(at, lanes) for lanes in (left, right) for at, _ in rank_places()]

    def chip_places():
        return [((chip_of() ^ k) * part, every) for k in range(chips)]

    def chip_places_both():
        me = core_of()
        own, other = [pl.ds(pl.multiple_of(who * row_half, row_half), row_half) for who in (me, 1 - me)]
        return [(at, own) for at, _ in chip_places()] + [(0, other)]

    def whole_place():
        return [(0, every)]

    def my_rows():
        return core_of() * row_half

    def other_rows():
        return (1 - core_of()) * row_half

    def to_rank(cuts):
        return [cuts[0]] + [swap(cuts[k], "rows", k) for k in range(1, depth_ranks)]

    def all_rows(x):
        return [x] + [swap(x, "rows", k) for k in range(1, depth_ranks)]

    a_pieces = None
    for step in range(STEPS):
        if step == 0:
            tile, theirs, mine = tile_and_logits(features, centers, a)
        else:
            theirs, mine = across(
                tile, a_pieces, rank_places_both, out, 0, rows_here, slice(0, count), "logits", halves=True, near=True
            )
        logits = add_up([mine, swap(theirs, "centers", 1)], "chip_logits")
        logits = [logits] + [swap(logits, "centers", 2 * k) for k in range(1, chips)]
        resid = residuals(logits, labels.T, rows_total)
        resids = [resid, swap(resid, "centers", 1)]
        grads = []
        for lanes, name in ((left, "grada"), (right, "gradb")):
            cuts = down(
                [tile],
                resids,
                core_places,
                out,
                0,
                rows_here,
                lanes,
                name,
                chunks=depth_ranks,
                near=lambda size, lanes=lanes: [(0, rows_here // size, 0, lanes)],
            )
            grads.append(all_rows(add_up(to_rank(cuts), "grad_sum")))
        places = rank_places
        if step == 0:
            begun, near_left = across(precond, grads[0], places, out, 0, p_rows, left, "fwda", keep=True)
            theirs, near_other = across(
                precond, grads[1], places, out, other_rows, row_half, right, "fwdb", before=begun, keep=True
            )
            mine, near_mine = across(
                precond, grads[1], places, out, my_rows, row_half, right, "fwdc", before=begun, keep=True
            )
        else:
            (begun,) = across(near_left, grads[0], places, out, 0, p_rows, left, "fwda", near=True)
            (theirs,) = across(
                near_other, grads[1], places, out, other_rows, row_half, right, "fwdb", before=begun, near=True
            )
            (mine,) = across(
                near_mine, grads[1], places, out, my_rows, row_half, right, "fwdc", before=begun, near=True
            )
        cuts = add_and_cut(mine, swap(theirs, "centers", 1), chips, "cut")
        fwd = add_up([cuts[0]] + [swap(cuts[k], "centers", 2 * k) for k in range(1, chips)], "fwd_sum")
        fwds = [fwd] + [swap(fwd, "centers", 2 * k) for k in range(1, chips)]
        others = [swap(assemble(fwds, chip_places, (out, row_half), "fwd_mine"), "centers", 1)]
        begun, squares = down(
            [near_left],
            fwds,
            chip_places,
            out,
            my_rows,
            row_half,
            left,
            "backa",
            squares="sum",
            near=lambda size: [(my_rows() // size, row_half // size, 0, every)],
        )
        cuts = down(
            [near_left],
            others,
            whole_place,
            out,
            other_rows,
            row_half,
            left,
            "backb",
            chunks=depth_ranks,
            before=begun,
            squares=squares,
            near=lambda size: [(other_rows() // size, row_half // size, 0, every)],
        )
        first, scale = update(to_rank(cuts), a_halves[0], center_total * out)
        cuts = down(
            [near_mine, near_other],
            fwds + others,
            chip_places_both,
            out,
            0,
            p_rows,
            right,
            "backc",
            chunks=depth_ranks,
            near=lambda size: [
                (0, row_half // size, my_rows(), every),
                (0, row_half // size, other_rows(), every),
            ],
        )
        (second,) = update(to_rank(cuts), a_halves[1], center_total * out, scale)
        a_halves = [first, second]
        a_pieces = all_rows(first) + all_rows(second)
    return assemble(a_pieces, rank_places_both, (out, count), "result").T


def plain_tile(rows_x, centers_x):
    width = rows_x.shape[1]
    left = jnp.sum(rows_x * rows_x, axis=1)
    right = jnp.sum(centers_x * centers_x, axis=1)
    cross = jnp.dot(rows_x, centers_x.T, precision=lax.Precision.HIGHEST)
    return jnp.exp(-2.0 * (left[:, None] + right[None, :] - 2.0 * cross) / width)


def plain_body(features, centers, labels, coeffs, precond):
    rows_total = features.shape[0] * lax.axis_size("rows")
    center_total = coeffs.shape[0] * lax.axis_size("centers")
    targets = labels.astype(f32)
    share_rows = features.shape[0] // lax.axis_size("centers")
    highest = lax.Precision.HIGHEST
    tile = plain_tile(features, centers)
    for step in range(STEPS):
        part = jnp.dot(tile, coeffs, precision=highest)
        share = lax.psum_scatter(part, "centers", scatter_dimension=0, tiled=True)
        offset = lax.axis_index("centers") * share_rows
        share_y = lax.dynamic_slice_in_dim(targets, offset, share_rows, 0)
        share_resid = (jax.nn.sigmoid(share) - share_y) / rows_total
        resid = lax.all_gather(share_resid, "centers", axis=0, tiled=True)
        grad = lax.psum(lax.dot_general(tile, resid, (((0,), (0,)), ((), ())), precision=highest), "rows")
        fwd = lax.psum(jnp.dot(precond, grad, precision=highest), "centers")
        back = lax.psum(lax.dot_general(precond, fwd, (((0,), (0,)), ((), ())), precision=highest), "rows")
        total = lax.psum(jnp.sum(fwd * fwd), "rows")
        scale = step_size / jnp.sqrt(total / (center_total * fwd.shape[1]) + epsilon)
        coeffs = coeffs - scale * back
    return coeffs


def fits(ranks, cols, features, coeffs, precond):
    if cols % 2 or ranks & (ranks - 1) or cols & (cols - 1):
        return False
    out = coeffs.shape[1]
    lanes = (features.shape[0] // ranks, coeffs.shape[0] // cols // 2, precond.shape[0] // ranks // 2)
    return out % (8 * ranks) == 0 and out % (4 * cols) == 0 and out % 16 == 0 and all(n % 128 == 0 for n in lanes)


def solution(mesh):
    in_specs = (
        P("rows", None),
        P("centers", None),
        P("rows", None),
        P("centers", None),
        P("rows", "centers"),
    )
    out_specs = P("centers", None)

    def program(features, centers, labels, coeffs, precond):
        fit = fits(mesh.shape["rows"], mesh.shape["centers"], features, coeffs, precond)
        one = jax.shard_map(
            body if fit else plain_body, mesh=mesh, in_specs=in_specs, out_specs=out_specs, check_vma=False
        )
        return one(features, centers, labels, coeffs, precond)

    return program
```

```python
import functools

import jax
import jax.numpy as jnp
from jax import lax
from jax.experimental import pallas as pl
from jax.experimental.pallas import tpu as pltpu
from jax.sharding import PartitionSpec as P

STEPS = 2
step_size = 0.5
epsilon = 1e-06

f32 = jnp.float32
bf16 = jnp.bfloat16
LOG2E = 1.4426950408889634
NN = (((1,), (0,)), ((), ()))
NT = (((1,), (1,)), ((), ()))
WHOLE = pl.BlockSpec(memory_space=pltpu.VMEM)
FAR = pl.BlockSpec(memory_space=pltpu.HBM)
VMEM_LIMIT = 13 << 20
TILE_LIMIT = 30 << 20
NEAR_LIMIT = 13 << 20
SMALL_LIMIT = 6 << 20
IN_FLIGHT = 6 << 20


def dot(a, b, dims):
    return lax.dot_general(a, b, dims, preferred_element_type=f32)


def split(x):
    high = x.astype(bf16)
    return high, (x - high.astype(f32)).astype(bf16)


def split3(x):
    high = x.astype(bf16)
    rest = x - high.astype(f32)
    mid = rest.astype(bf16)
    return high, mid, (rest - mid.astype(f32)).astype(bf16)


def core_of():
    return lax.rem(lax.axis_index("centers"), 2)


def chip_of():
    return lax.div(lax.axis_index("centers"), 2)


def rows_at(start, count):
    if isinstance(start, int):
        return pl.ds(start, count)
    return pl.ds(pl.multiple_of(start, count), count)


def stage(pieces, places, full, parts):
    for piece, (start, lanes) in zip(pieces, places()):
        full[rows_at(start, piece.shape[0]), lanes] = piece[...]
    high, low = split(full[...])
    out = full.shape[0]
    parts[0:out] = high
    parts[out : 2 * out] = low


def block_of(total, most):
    size = min(total, most)
    while total % size:
        size //= 2
    return size


def offset(first, size):
    return first if isinstance(first, int) else pl.multiple_of(first(), size)


def stream(w_ref, held, sems, first, count, size, lanes, use):
    blocks = count // size
    start = offset(first, size)

    def at(i):
        return pl.ds(pl.multiple_of(i * size, size), size)

    def rows(i):
        return pl.ds(pl.multiple_of(start + i * size, size), size)

    def copy(i, slot):
        return pltpu.make_async_copy(w_ref.at[rows(i), lanes], held.at[slot], sems.at[slot])

    slots = min(held.shape[0], blocks)
    for i in range(slots):
        copy(i, i).start()

    def one(i, carry):
        slot = lax.rem(i, slots)
        copy(i, slot).wait()
        use(at(i), held[slot])

        @pl.when(i + slots < blocks)
        def _():
            copy(i + slots, slot).start()

        return carry

    lax.fori_loop(0, blocks, one, 0)


def stream_near(sources, size, use):
    for ref, first, count, at, lanes in sources:

        def one(i, carry, ref=ref, first=first, at=at, lanes=lanes):
            use(pl.ds(pl.multiple_of(at + i * size, size), size), ref[first + i, :, lanes])
            return carry

        lax.fori_loop(0, count, one, 0)


def call(kernel, weights, others, outs, scratch, count, size, n_lanes, out, name, limit, near=False, keep=False):
    weights = list(weights) if near else [weights]
    n_weights, n_in, n_out, n_scratch = len(weights), len(others), len(outs), len(scratch)

    def whole(*refs):
        ins, rest = refs[n_weights : n_weights + n_in], refs[n_weights + n_in :]
        if near:
            held = sems = None
        elif keep:
            held, sems = rest[n_out], rest[-1]
        else:
            held, sems = rest[n_out + n_scratch :]
        first = n_out + (1 if keep else 0)
        kernel(refs[:n_weights], ins, rest[:n_out], rest[first : first + n_scratch], held, sems)

    slots = max(2, min(count // size, IN_FLIGHT // (4 * size * n_lanes)))
    scratch = list(scratch)
    outs = list(outs)
    if keep:
        slots = count // size
        outs.append((slots, size, n_lanes))
    elif not near:
        scratch.append(pltpu.VMEM((slots, size, n_lanes), f32))
    if not near:
        scratch.append(pltpu.SemaphoreType.DMA((slots,)))
    return pl.pallas_call(
        whole,
        in_specs=[WHOLE if near else FAR] * n_weights + [WHOLE] * n_in,
        out_specs=[WHOLE] * len(outs),
        out_shape=[jax.ShapeDtypeStruct(shape, f32) for shape in outs],
        scratch_shapes=scratch,
        compiler_params=pltpu.CompilerParams(vmem_limit_bytes=limit),
        cost_estimate=pl.CostEstimate(
            flops=6 * out * count * n_lanes, bytes_accessed=4 * count * n_lanes, transcendentals=0
        ),
        name=name,
    )(*weights, *others)


def down(weights, pieces, places, out, first, count, lanes, name, chunks=0, before=None, squares=None, limit=VMEM_LIMIT, near=None):
    size = block_of(count, 512)
    n_lanes = lanes.stop - lanes.start
    n_pieces = len(pieces)
    share = out // chunks if chunks else out
    gives = isinstance(squares, str)
    takes = squares is not None and not gives
    extra = 128 if takes else 0
    others = list(pieces) + ([before] if before is not None else []) + ([squares] if takes else [])
    outs = [(share, n_lanes + extra)] * (chunks or 1) + ([(8, 128)] if gives else [])

    def kernel(w_ref, ins, out_refs, scratch, held, sems):
        full, parts, total = scratch

        def use(at, block):
            x = parts[:, at]
            high, low = split(block)
            both = dot(x, high, NN)
            total[...] += both[:out] + both[out:] + dot(x[:out], low, NN)

        total[...] = jnp.zeros_like(total) if before is None else ins[n_pieces][...]
        stage(ins[:n_pieces], places, full, parts)
        if near is None:
            stream(w_ref[0], held, sems, first, count, size, lanes, use)
        else:
            stream_near([(ref, *rest) for ref, rest in zip(w_ref, near(size))], size, use)
        if not chunks:
            out_refs[0][...] = total[...]
        for k in range(chunks):
            at = rows_at((lax.axis_index("rows") ^ k) * share, share)
            out_refs[k][:, 0:n_lanes] = total[at, :]
        if gives:
            out_refs[-1][...] = jnp.full((8, 128), jnp.sum(full[...] * full[...]), f32)
        if takes:
            sum_sq = jnp.sum(full[...] * full[...]) + jnp.max(ins[-1][0:1, :])
            for k in range(chunks):
                out_refs[k][:, n_lanes : n_lanes + extra] = jnp.full((share, extra), sum_sq, f32)

    scratch = [pltpu.VMEM((out, count), f32), pltpu.VMEM((2 * out, count), bf16), pltpu.VMEM((out, n_lanes), f32)]
    return call(kernel, weights, others, outs, scratch, count, size, n_lanes, out, name, limit, near is not None)


def across(weights, pieces, places, out, first, count, lanes, name, before=None, halves=False, limit=VMEM_LIMIT, near=False, keep=False):
    width = lanes.stop - lanes.start
    size = block_of(count, 512)
    weights = [weights] if near else weights
    half = out // 2
    n_pieces = len(pieces)
    outs = [(half, count)] * 2 if halves else [(out, count)]
    others = list(pieces) + ([before] if before is not None else [])

    def kernel(w_ref, ins, out_refs, scratch, held, sems):
        full, parts = scratch[:2]
        total = scratch[2] if halves else out_refs[0]

        def use(at, block):
            high, low = split(block)
            both = dot(parts[...], high, NT)
            sums = both[:out] + both[out:] + dot(parts[0:out], low, NT)
            if before is not None:
                sums = sums + ins[n_pieces][:, pl.ds(pl.multiple_of(offset(first, size) + at.start, size), size)]
            total[:, at] = sums

        stage(ins[:n_pieces], places, full, parts)
        if near:
            stream_near([(w_ref[0], 0, count // size, 0, slice(None))], size, use)
        else:
            stream(w_ref[0], held, sems, first, count, size, lanes, use)
        if halves:
            core = core_of()
            out_refs[0][...] = total[rows_at((1 - core) * half, half), :]
            out_refs[1][...] = total[rows_at(core * half, half), :]

    scratch = [pltpu.VMEM((out, width), f32), pltpu.VMEM((2 * out, width), bf16)]
    scratch += [pltpu.VMEM((out, count), f32)] if halves else []
    return call(kernel, weights, others, outs, scratch, count, size, width, out, name, limit, near, keep)


def tile_and_logits(features, centers, coeffs):
    rows, width = features.shape
    count = centers.shape[0]
    out = coeffs.shape[0]
    half = out // 2
    size = block_of(rows, 512)
    gain = 2.0 * LOG2E / width

    def kernel(x_ref, c_ref, a_ref, tile_ref, theirs, mine, wide, norms, parts, total):
        @pl.when(pl.program_id(0) == 0)
        def _():
            c = c_ref[...]
            high, mid, low = split3(c * (2.0 * gain))
            wide[...] = jnp.concatenate([high, high, mid, mid, low, high], axis=1)
            norms[...] = lax.dot_general(
                jnp.full((8, width), gain, f32),
                c * c,
                NT,
                precision=lax.Precision.HIGHEST,
                preferred_element_type=f32,
            )
            high, low = split(a_ref[...])
            parts[0:out] = high
            parts[out : 2 * out] = low

        x = x_ref[...]
        high, mid, low = split3(x)
        cross = dot(jnp.concatenate([high, mid, high, mid, high, low], axis=1), wide[...], NT)
        norm = jnp.sum(x * x, axis=1, keepdims=True) * gain
        tile = jnp.exp2((cross - norm) - norms[0:1, :])
        tile_ref[0] = tile
        high, low = split(tile)
        both = dot(parts[...], high, NT)
        total[...] = both[:out] + both[out:] + dot(parts[0:out], low, NT)
        core = core_of()
        theirs[...] = total[rows_at((1 - core) * half, half), :]
        mine[...] = total[rows_at(core * half, half), :]

    return pl.pallas_call(
        kernel,
        grid=(rows // size,),
        in_specs=[
            pl.BlockSpec((size, width), lambda i: (i, 0)),
            pl.BlockSpec((count, width), lambda i: (0, 0)),
            pl.BlockSpec((out, count), lambda i: (0, 0)),
        ],
        out_specs=[
            pl.BlockSpec((1, size, count), lambda i: (i, 0, 0)),
            pl.BlockSpec((half, size), lambda i: (0, i)),
            pl.BlockSpec((half, size), lambda i: (0, i)),
        ],
        out_shape=[
            jax.ShapeDtypeStruct((rows // size, size, count), f32),
            jax.ShapeDtypeStruct((half, rows), f32),
            jax.ShapeDtypeStruct((half, rows), f32),
        ],
        scratch_shapes=[
            pltpu.VMEM((count, 6 * width), bf16),
            pltpu.VMEM((8, count), f32),
            pltpu.VMEM((2 * out, count), bf16),
            pltpu.VMEM((out, size), f32),
        ],
        compiler_params=pltpu.CompilerParams(vmem_limit_bytes=TILE_LIMIT),
        cost_estimate=pl.CostEstimate(
            flops=12 * rows * width * count, bytes_accessed=4 * rows * count, transcendentals=rows * count
        ),
        name="tile_and_logits",
    )(features, centers, coeffs)


def add_and_cut(first, second, chips, name):
    rows, count = first.shape
    share = rows // chips

    def kernel(a_ref, b_ref, *outs):
        chip = chip_of()
        for k in range(chips):
            at = rows_at((chip ^ k) * share, share)
            outs[k][...] = a_ref[at, :] + b_ref[at, :]

    return pl.pallas_call(
        kernel,
        in_specs=[WHOLE] * 2,
        out_specs=[WHOLE] * chips,
        out_shape=[jax.ShapeDtypeStruct((share, count), f32)] * chips,
        compiler_params=pltpu.CompilerParams(vmem_limit_bytes=SMALL_LIMIT),
        name=name,
    )(first, second)


def small(kernel, others, outs, name):
    return pl.pallas_call(
        kernel,
        in_specs=[WHOLE] * len(others),
        out_specs=[WHOLE] * len(outs),
        out_shape=[jax.ShapeDtypeStruct(shape, f32) for shape in outs],
        compiler_params=pltpu.CompilerParams(vmem_limit_bytes=SMALL_LIMIT),
        name=name,
    )(*others)


def add_up(terms, name):
    def kernel(*refs):
        total = refs[0][...]
        for ref in refs[1:-1]:
            total = total + ref[...]
        refs[-1][...] = total

    return small(kernel, terms, [terms[0].shape], name)[0]


def residuals(logits, labels, rows_total):
    half = logits[0].shape[0]

    def kernel(*refs):
        total = refs[0][...]
        for ref in refs[1:-2]:
            total = total + ref[...]
        targets = refs[-2][rows_at(core_of() * half, half), :].astype(f32)
        refs[-1][...] = (jax.nn.sigmoid(total) - targets) / rows_total

    return small(kernel, [*logits, labels], [logits[0].shape], "resid")[0]


def rank_share(a, share, lanes):
    def kernel(a_ref, *outs):
        at = rows_at(lax.axis_index("rows") * share, share)
        for out, cut in zip(outs, lanes):
            out[...] = a_ref[at, cut]

    return small(kernel, [a], [(share, cut.stop - cut.start) for cut in lanes], "share")


def update(cuts, a, elements, scale=None):
    rows, count = a.shape
    n_cuts = len(cuts)

    def kernel(*refs):
        back = refs[0][...]
        for ref in refs[1:n_cuts]:
            back = back + ref[...]
        if scale is None:
            step = step_size / jnp.sqrt(back[0:8, count:] / elements + epsilon)
            refs[-1][...] = step
        else:
            step = refs[n_cuts + 1][...]
        refs[n_cuts + (1 if scale is None else 2)][...] = refs[n_cuts][...] - step[0:1, 0:1] * back[:, 0:count]

    return pl.pallas_call(
        kernel,
        in_specs=[WHOLE] * (n_cuts + (1 if scale is None else 2)),
        out_specs=[WHOLE] * (2 if scale is None else 1),
        out_shape=[jax.ShapeDtypeStruct((rows, count), f32)] + ([jax.ShapeDtypeStruct((8, 128), f32)] if scale is None else []),
        compiler_params=pltpu.CompilerParams(vmem_limit_bytes=SMALL_LIMIT),
        name="update",
    )(*cuts, a, *([] if scale is None else [scale]))


def assemble(pieces, places, shape, name):
    n_pieces = len(pieces)

    def kernel(*refs):
        for piece, (start, lanes) in zip(refs[:n_pieces], places()):
            refs[n_pieces][rows_at(start, piece.shape[0]), lanes] = piece[...]

    return pl.pallas_call(
        kernel,
        in_specs=[WHOLE] * n_pieces,
        out_specs=WHOLE,
        out_shape=jax.ShapeDtypeStruct(shape, f32),
        compiler_params=pltpu.CompilerParams(vmem_limit_bytes=SMALL_LIMIT),
        name=name,
    )(*pieces)


def swap(x, axis, mask):
    size = lax.axis_size(axis)
    return lax.ppermute(x, axis, [(i, i ^ mask) for i in range(size)])


def body(features, centers, labels, coeffs, precond):
    depth_ranks = lax.axis_size("rows")
    chips = lax.axis_size("centers") // 2
    rows_here = features.shape[0]
    rows_total = rows_here * depth_ranks
    count, out = coeffs.shape
    center_total = count * lax.axis_size("centers")
    half = out // 2
    share = out // depth_ranks
    part = out // chips
    cols = count // 2
    row_half = precond.shape[0] // 2
    p_rows = precond.shape[0]
    left, right = slice(0, cols), slice(cols, count)
    every = slice(None)

    a = coeffs.T
    a_halves = rank_share(a, share, (left, right))

    def core_places():
        me = core_of()
        return [(me * half, every), ((1 - me) * half, every)]

    def rank_places():
        return [((lax.axis_index("rows") ^ k) * share, every) for k in range(depth_ranks)]

    def rank_places_both():
        return [(at, lanes) for lanes in (left, right) for at, _ in rank_places()]

    def chip_places():
        return [((chip_of() ^ k) * part, every) for k in range(chips)]

    def chip_places_both():
        me = core_of()
        own, other = [pl.ds(pl.multiple_of(who * row_half, row_half), row_half) for who in (me, 1 - me)]
        return [(at, own) for at, _ in chip_places()] + [(0, other)]

    def whole_place():
        return [(0, every)]

    def my_rows():
        return core_of() * row_half

    def other_rows():
        return (1 - core_of()) * row_half

    def to_rank(cuts):
        return [cuts[0]] + [swap(cuts[k], "rows", k) for k in reversed(range(1, depth_ranks))]

    def all_rows(x):
        far_first = [swap(x, "rows", k) for k in reversed(range(1, depth_ranks))]
        return [x] + far_first[::-1]

    a_pieces = None
    for step in range(STEPS):
        if step == 0:
            tile, theirs, mine = tile_and_logits(features, centers, a)
        else:
            theirs, mine = across(
                tile, a_pieces, rank_places_both, out, 0, rows_here, slice(0, count), "logits", halves=True, near=True
            )
        logits = add_up([mine, swap(theirs, "centers", 1)], "chip_logits")
        logits = [logits] + [swap(logits, "centers", 2 * k) for k in range(1, chips)]
        resid = residuals(logits, labels.T, rows_total)
        resids = [resid, swap(resid, "centers", 1)]
        grads = []
        for lanes, name in ((left, "grada"), (right, "gradb")):
            cuts = down(
                [tile],
                resids,
                core_places,
                out,
                0,
                rows_here,
                lanes,
                name,
                chunks=depth_ranks,
                near=lambda size, lanes=lanes: [(0, rows_here // size, 0, lanes)],
            )
            grads.append(all_rows(add_up(to_rank(cuts), "grad_sum")))
        places = rank_places
        if step == 0:
            begun, near_left = across(precond, grads[0], places, out, 0, p_rows, left, "fwda", keep=True)
            theirs, near_other = across(
                precond, grads[1], places, out, other_rows, row_half, right, "fwdb", before=begun, keep=True
            )
            mine, near_mine = across(
                precond, grads[1], places, out, my_rows, row_half, right, "fwdc", before=begun, keep=True
            )
        else:
            (begun,) = across(near_left, grads[0], places, out, 0, p_rows, left, "fwda", near=True)
            (theirs,) = across(
                near_other, grads[1], places, out, other_rows, row_half, right, "fwdb", before=begun, near=True
            )
            (mine,) = across(
                near_mine, grads[1], places, out, my_rows, row_half, right, "fwdc", before=begun, near=True
            )
        cuts = add_and_cut(mine, swap(theirs, "centers", 1), chips, "cut")
        fwd = add_up([cuts[0]] + [swap(cuts[k], "centers", 2 * k) for k in range(1, chips)], "fwd_sum")
        fwds = [fwd] + [swap(fwd, "centers", 2 * k) for k in range(1, chips)]
        others = [swap(assemble(fwds, chip_places, (out, row_half), "fwd_mine"), "centers", 1)]
        begun, squares = down(
            [near_left],
            fwds,
            chip_places,
            out,
            my_rows,
            row_half,
            left,
            "backa",
            squares="sum",
            near=lambda size: [(my_rows() // size, row_half // size, 0, every)],
        )
        cuts = down(
            [near_left],
            others,
            whole_place,
            out,
            other_rows,
            row_half,
            left,
            "backb",
            chunks=depth_ranks,
            before=begun,
            squares=squares,
            near=lambda size: [(other_rows() // size, row_half // size, 0, every)],
        )
        first, scale = update(to_rank(cuts), a_halves[0], center_total * out)
        cuts = down(
            [near_mine, near_other],
            fwds + others,
            chip_places_both,
            out,
            0,
            p_rows,
            right,
            "backc",
            chunks=depth_ranks,
            near=lambda size: [
                (0, row_half // size, my_rows(), every),
                (0, row_half // size, other_rows(), every),
            ],
        )
        (second,) = update(to_rank(cuts), a_halves[1], center_total * out, scale)
        a_halves = [first, second]
        a_pieces = all_rows(first) + all_rows(second)
    return assemble(a_pieces, rank_places_both, (out, count), "result").T


def plain_tile(rows_x, centers_x):
    width = rows_x.shape[1]
    left = jnp.sum(rows_x * rows_x, axis=1)
    right = jnp.sum(centers_x * centers_x, axis=1)
    cross = jnp.dot(rows_x, centers_x.T, precision=lax.Precision.HIGHEST)
    return jnp.exp(-2.0 * (left[:, None] + right[None, :] - 2.0 * cross) / width)


def plain_body(features, centers, labels, coeffs, precond):
    rows_total = features.shape[0] * lax.axis_size("rows")
    center_total = coeffs.shape[0] * lax.axis_size("centers")
    targets = labels.astype(f32)
    share_rows = features.shape[0] // lax.axis_size("centers")
    highest = lax.Precision.HIGHEST
    tile = plain_tile(features, centers)
    for step in range(STEPS):
        part = jnp.dot(tile, coeffs, precision=highest)
        share = lax.psum_scatter(part, "centers", scatter_dimension=0, tiled=True)
        offset = lax.axis_index("centers") * share_rows
        share_y = lax.dynamic_slice_in_dim(targets, offset, share_rows, 0)
        share_resid = (jax.nn.sigmoid(share) - share_y) / rows_total
        resid = lax.all_gather(share_resid, "centers", axis=0, tiled=True)
        grad = lax.psum(lax.dot_general(tile, resid, (((0,), (0,)), ((), ())), precision=highest), "rows")
        fwd = lax.psum(jnp.dot(precond, grad, precision=highest), "centers")
        back = lax.psum(lax.dot_general(precond, fwd, (((0,), (0,)), ((), ())), precision=highest), "rows")
        total = lax.psum(jnp.sum(fwd * fwd), "rows")
        scale = step_size / jnp.sqrt(total / (center_total * fwd.shape[1]) + epsilon)
        coeffs = coeffs - scale * back
    return coeffs


def fits(ranks, cols, features, coeffs, precond):
    if cols % 2 or ranks & (ranks - 1) or cols & (cols - 1):
        return False
    out = coeffs.shape[1]
    lanes = (features.shape[0] // ranks, coeffs.shape[0] // cols // 2, precond.shape[0] // ranks // 2)
    return out % (8 * ranks) == 0 and out % (4 * cols) == 0 and out % 16 == 0 and all(n % 128 == 0 for n in lanes)


def solution(mesh):
    in_specs = (
        P("rows", None),
        P("centers", None),
        P("rows", None),
        P("centers", None),
        P("rows", "centers"),
    )
    out_specs = P("centers", None)

    def program(features, centers, labels, coeffs, precond):
        fit = fits(mesh.shape["rows"], mesh.shape["centers"], features, coeffs, precond)
        one = jax.shard_map(
            body if fit else plain_body, mesh=mesh, in_specs=in_specs, out_specs=out_specs, check_vma=False
        )
        return one(features, centers, labels, coeffs, precond)

    return program
```
